32 devices in a mesh: recon: 1, slab: 32 (over z, y, x, core), coil: 1.
Axes of the slice: x: 2, y: 2, z: 4, core: 2. Of those that a mesh axis runs over, the one named last changes fastest.
Arguments:
- image: float32 [2, 192, 192, 192], P('recon', 'slab'), may hold values from -6 to 6
- prox_point: float32 [2, 192, 192, 192], P('recon', 'slab'), may hold values from -6 to 6
- dual: float32 [2, 192, 192, 192], P('recon', 'slab'), may hold values from -6 to 6
- adjoint_data: float32 [2, 192, 192, 192], P('recon', 'slab'), may hold values from -6 to 6
- coil_maps: float32 [1, 2, 192, 192, 192], P('coil', 'recon', 'slab'), may hold values from -4 to 4
- kernel: float32 [384, 384, 384], P('slab'), may hold values from 0.05 to 5
Outputs:
- image_new: float32 [2, 192, 192, 192], P('recon', 'slab')
- prox_new: float32 [2, 192, 192, 192], P('recon', 'slab')
- dual_new: float32 [2, 192, 192, 192], P('recon', 'slab')
The draws below stay inside these ranges and needn't reach their ends.
All inputs are finite; a program needn't handle non-finite values.
Results may differ from the reference program's by a relative error of at most 0.00015.
Values sent between devices are 32-bit elements; how exact they have to be, the bound alone decides.
No kernel may reach another device: no remote copies, remote signals or barrier semaphores. Data moves between devices by JAX's collectives and lax.ppermute only.
A program may use at most 192 MiB of HBM per device.

```python
import math
import jax
import jax.numpy as jnp

IMG = 192
GRID = 384
COILS = 1


def steps_of(stream_key, dims, shards, smallest, top_value):
    def one(dim, parts):
        steps = jax.random.uniform(jax.random.fold_in(jax.random.fold_in(stream_key, 6), dim), (parts,), jnp.float32, smallest / len(shards), top_value / len(shards))
        return jnp.repeat(jnp.exp(steps), dims[dim] // parts).reshape((-1,) + (1,) * (len(dims) - dim - 1))

    gain = one(*shards[0])
    for cut in shards[1:]:
        gain = gain * one(*cut)
    return gain


def noise(stream_key, dims, spread, reach, shards=(), kind=jnp.bfloat16):
    gain = steps_of(stream_key, dims, shards, -0.22, 0.18) if shards else 1.0
    array = jax.random.normal(stream_key, dims, jnp.float32) * spread * gain
    return jnp.minimum(jnp.maximum(array, -reach), reach).astype(kind)


def setup_inputs(seed: int = 0, part: int = 0) -> dict:
    arg_keys = jax.random.split(jax.random.key(seed), 7)
    part_splits = jax.random.split(jax.random.fold_in(arg_keys[6], part), 7)
    image = noise(part_splits[0], (2, IMG, IMG, IMG), 1.0, 6.0, ((1, 32),), jnp.float32)
    prox_point = noise(part_splits[1], (2, IMG, IMG, IMG), 1.0, 6.0, ((1, 32),), jnp.float32)
    dual = noise(part_splits[2], (2, IMG, IMG, IMG), 0.5, 6.0, ((1, 32),), jnp.float32)
    adjoint_data = noise(part_splits[3], (2, IMG, IMG, IMG), 1.0, 6.0, ((1, 32),), jnp.float32)
    coil_maps = noise(part_splits[4], (COILS, 2, IMG, IMG, IMG), (2 * COILS) ** -0.5, 4.0, ((2, 32),), jnp.float32)
    kernel = jnp.clip(jnp.exp(math.log(5.0) - 4.6051702 * jax.random.uniform(arg_keys[5], (GRID, GRID, GRID), jnp.float32) ** steps_of(arg_keys[5], (GRID, GRID, GRID), ((0, 32),), -0.2, 0.2)), 0.05, 5.0)
    return dict(image=image, prox_point=prox_point, dual=dual, adjoint_data=adjoint_data, coil_maps=coil_maps, kernel=kernel)


half_root = 0.7071067811865476
shrink = 0.5
step_size = 0.25
penalty = 1.0

def pair_axis(values, axis_dim, offset):
    length = values.shape[axis_dim]
    layout = [1] * values.ndim
    layout[axis_dim] = length
    is_first = ((jnp.arange(length) - offset) % 2 == 0).reshape(layout)
    after_one = jnp.roll(values, -1, axis_dim)
    before_one = jnp.roll(values, 1, axis_dim)
    return jnp.where(is_first, (values + after_one) * half_root, (before_one - values) * half_root)

def first_mask(length, offset):
    return (jnp.arange(length) - offset) % 2 == 0

def spin(field, offset):
    coefs = field
    for axis_dim in (1, 2, 3):
        coefs = pair_axis(coefs, axis_dim, offset)
    keep = first_mask(field.shape[1], offset)[:, None, None] & first_mask(field.shape[2], offset)[None, :, None] & first_mask(field.shape[3], offset)[None, None, :]
    magnitude = jnp.sqrt(coefs[0] * coefs[0] + coefs[1] * coefs[1])
    factor = jnp.maximum(magnitude - shrink, 0.0) / jnp.maximum(magnitude, shrink)
    coefs = jnp.where(keep[None], coefs, coefs * factor[None])
    for axis_dim in (3, 2, 1):
        coefs = pair_axis(coefs, axis_dim, offset)
    return coefs

def reference(image, prox_point, dual, adjoint_data, coil_maps, kernel):
    picture = image[0] + 1j * image[1]
    spectrum_gain = jnp.transpose(kernel, (2, 0, 1))
    normal = jnp.zeros(picture.shape, picture.dtype)
    for coil_index in range(COILS):
        profile = coil_maps[coil_index, 0] + 1j * coil_maps[coil_index, 1]
        padded = jnp.pad(profile * picture, ((0, GRID - IMG), (0, GRID - IMG), (0, GRID - IMG)))
        filtered = jnp.fft.ifftn(jnp.fft.fftn(padded) * spectrum_gain)[:IMG, :IMG, :IMG]
        normal = normal + jnp.conj(profile) * filtered
    normal_parts = jnp.stack([jnp.real(normal), jnp.imag(normal)]).astype(image.dtype)
    image_new = image - step_size * (normal_parts - adjoint_data + penalty * (image - prox_point + dual))
    merged = image_new + dual
    prox_new = 0.5 * (spin(merged, 0) + spin(merged, 1))
    dual_new = dual + image_new - prox_new
    return (image_new, prox_new, dual_new)
```

```python
import functools
import math

import jax
import jax.numpy as jnp
import ml_dtypes
import numpy as np
from jax import lax
from jax.experimental import pallas as pl
from jax.experimental.pallas import tpu as pltpu
from jax.sharding import PartitionSpec as P

half_root = 0.7071067811865476
shrink = 0.5
step_size = 0.25
penalty = 1.0
VMEM_LIMIT = 56 * 1024 * 1024


def real_form(rows, cols, length, direction, gain=1.0):
    angle = 2.0 * math.pi / length * (np.outer(rows, cols) % length).astype(np.float64)
    cosine = np.cos(angle) * gain
    sine = direction * np.sin(angle) * gain
    return np.concatenate(
        [np.concatenate([cosine, sine], 1), np.concatenate([-sine, cosine], 1)], 0
    )


def three_way(table, axis):
    high = table.astype(ml_dtypes.bfloat16)
    low = (table - high.astype(np.float64)).astype(ml_dtypes.bfloat16)
    return np.concatenate([high, high, low], axis)


def split(values):
    high = values.astype(jnp.bfloat16)
    low = (values - high.astype(jnp.float32)).astype(jnp.bfloat16)
    return high, low


def stacked(parts, axis):
    pairs = [split(part) for part in parts]
    highs = [pair[0] for pair in pairs]
    lows = [pair[1] for pair in pairs]
    return jnp.concatenate(highs + lows + highs, axis=axis)


def product(left, right):
    return jnp.dot(left, right, preferred_element_type=jnp.float32)


def spread_kernel(image_ref, coil_ref, table_ref, *out_refs):
    planes = image_ref.shape[1]
    reals, imags = [], []
    for plane in range(planes):
        img_r, img_i = image_ref[0, plane], image_ref[1, plane]
        map_r, map_i = coil_ref[0, plane], coil_ref[1, plane]
        reals.append(map_r * img_r - map_i * img_i)
        imags.append(map_r * img_i + map_i * img_r)
    right = stacked([jnp.concatenate(reals, axis=1), jnp.concatenate(imags, axis=1)], 0)
    for chunk, out_ref in enumerate(out_refs):
        out_ref[...] = product(table_ref[chunk], right)


def middle_kernel(count, planes, steps, data_ref, gain_ref, fx_ref, fz_ref, gz_ref, gx_ref, out_ref, came, goes):
    step = pl.program_id(0)
    lanes = data_ref.shape[1]
    width = lanes // planes
    stride = data_ref.shape[0] // count
    grid_len = gain_ref.shape[1]
    depth = count * planes
    tiles = [(tile, min(128, lanes - tile * 128)) for tile in range(came.shape[0])]

    @pl.when(step == 0)
    def _():
        for tile, size in tiles:
            came[tile, :, :size] = data_ref[:, tile * 128 : tile * 128 + size]

    def part_of(part):
        pick = pl.ds(2 * step + part, count, stride=stride)
        rows = jnp.concatenate([came[tile, pick, :] for tile, _ in tiles], axis=1)
        return jnp.concatenate(
            [rows[:, plane * width : (plane + 1) * width] for plane in range(planes)], axis=0
        )

    left = stacked([part_of(0), part_of(1)], 1)
    along_x = product(left, fx_ref[...])
    right = stacked([along_x[:, :grid_len], along_x[:, grid_len:]], 0)
    spectrum = product(fz_ref[...], right)
    gain = gain_ref[0]
    right = stacked([spectrum[:grid_len] * gain, spectrum[grid_len:] * gain], 0)
    along_x = product(gz_ref[...], right)
    left = stacked([along_x[:depth], along_x[depth:]], 1)
    cells = product(left, gx_ref[...])
    for part in range(2):
        rows = jnp.concatenate(
            [
                cells[plane * count : (plane + 1) * count, part * width : (part + 1) * width]
                for plane in range(planes)
            ],
            axis=1,
        )
        pick = pl.ds(2 * step + part, count, stride=stride)
        for tile, size in tiles:
            goes[tile, pick, :] = jnp.pad(
                rows[:, tile * 128 : tile * 128 + size], ((0, 0), (0, 128 - size))
            )

    @pl.when(step == steps - 1)
    def _():
        for tile, size in tiles:
            out_ref[:, tile * 128 : tile * 128 + size] = goes[tile, :, :size]


def gather_kernel(chunks, *refs):
    data_refs = refs[:chunks]
    coil_ref, table_ref, out_ref = refs[chunks:]
    planes, height, width = coil_ref.shape[1:]
    field = product(table_ref[0], stacked([data_refs[0][...]], 0))
    for chunk in range(1, chunks):
        field = field + product(table_ref[chunk], stacked([data_refs[chunk][...]], 0))
    for plane in range(planes):
        real = field[:height, plane * width : (plane + 1) * width]
        imag = field[height:, plane * width : (plane + 1) * width]
        map_r, map_i = coil_ref[0, plane], coil_ref[1, plane]
        out_ref[0, plane] = map_r * real + map_i * imag
        out_ref[1, plane] = map_r * imag - map_i * real


def call(kernel, out_shape, **extra):
    return pl.pallas_call(
        kernel,
        out_shape=out_shape,
        compiler_params=pltpu.CompilerParams(vmem_limit_bytes=VMEM_LIMIT),
        **extra,
    )


def extended_2(cells, sides, width):
    for axis, dim in sides:
        count = lax.axis_size(axis)
        head = lax.slice_in_dim(cells, 0, width, axis=dim)
        tail = lax.slice_in_dim(cells, cells.shape[dim] - width, cells.shape[dim], axis=dim)
        cells = jnp.concatenate(
            [
                lax.ppermute(tail, axis, [(i, (i + 1) % count) for i in range(count)]),
                cells,
                lax.ppermute(head, axis, [((i + 1) % count, i) for i in range(count)]),
            ],
            axis=dim,
        )
    return cells


def pair_local(values, axis_dim, offset):
    length = values.shape[axis_dim]
    layout = [1] * values.ndim
    layout[axis_dim] = length
    is_first = ((jnp.arange(length) - offset) % 2 == 0).reshape(layout)
    after_one = jnp.roll(values, -1, axis_dim)
    before_one = jnp.roll(values, 1, axis_dim)
    return jnp.where(is_first, (values + after_one) * half_root, (before_one - values) * half_root)


def pair_planes(extended, own_first):
    middle = extended[:, 1:-1]
    after_one = extended[:, 2:]
    before_one = extended[:, :-2]
    marked = own_first[None, :, None, None]
    return jnp.where(marked, (middle + after_one) * half_root, (before_one - middle) * half_root)


def spin(extended, base, offset):
    total_planes = extended.shape[1]
    global_plane = base - 1 + jnp.arange(total_planes, dtype=jnp.int32)
    plane_first = (global_plane - offset) % 2 == 0
    own_first = plane_first[1:-1]
    lower_rim = (extended[:, :1] + extended[:, 1:2]) * half_root
    upper_rim = (extended[:, -2:-1] - extended[:, -1:]) * half_root
    coefs = jnp.concatenate([lower_rim, pair_planes(extended, own_first), upper_rim], axis=1)
    coefs = pair_local(coefs, 2, offset)
    coefs = pair_local(coefs, 3, offset)
    rows_first = (jnp.arange(extended.shape[2]) - offset) % 2 == 0
    cols_first = (jnp.arange(extended.shape[3]) - offset) % 2 == 0
    keep = plane_first[:, None, None] & rows_first[None, :, None] & cols_first[None, None, :]
    magnitude = jnp.sqrt(coefs[0] * coefs[0] + coefs[1] * coefs[1])
    factor = jnp.maximum(magnitude - shrink, 0.0) / jnp.maximum(magnitude, shrink)
    coefs = jnp.where(keep[None], coefs, coefs * factor[None])
    coefs = pair_local(coefs, 3, offset)
    coefs = pair_local(coefs, 2, offset)
    return pair_planes(coefs, own_first)


def filtered_normal(image, coil_map, gain_zx):
    count = lax.axis_size("slab")
    lines, grid_len = gain_zx.shape[:2]
    planes, height, width = image.shape[1:]
    depth = count * planes
    per_chunk = 4 if lines % 4 == 0 else lines
    chunks = lines // per_chunk
    rows = count * per_chunk * 2
    lanes = planes * width
    freq = np.arange(grid_len)

    def y_order(table, axis):
        shape = (2, count, chunks, per_chunk)
        order = np.arange(2 * grid_len).reshape(shape).transpose(2, 1, 3, 0).reshape(chunks, rows)
        return [np.take(table, part, axis) for part in order]

    forward_y = real_form(np.arange(height), freq, grid_len, -1.0).T
    forward_y = np.stack([three_way(part, 1) for part in y_order(forward_y, 0)])
    back_y = real_form(freq, np.arange(height), grid_len, 1.0, 1.0 / grid_len).T
    back_y = np.stack([three_way(part, 1) for part in y_order(back_y, 1)])
    z_order = np.arange(depth).reshape(count, planes).T.reshape(depth)
    forward_z = three_way(real_form(z_order, freq, grid_len, -1.0).T, 1)
    back_z = three_way(real_form(freq, z_order, grid_len, 1.0, 1.0 / grid_len).T, 1)
    forward_x = three_way(real_form(np.arange(width), freq, grid_len, -1.0), 0)
    back_x = three_way(real_form(freq, np.arange(width), grid_len, 1.0, 1.0 / grid_len), 0)

    flat = jax.ShapeDtypeStruct((rows, lanes), jnp.float32)
    sent = call(spread_kernel, [flat] * chunks)(image, coil_map, forward_y)

    whole = lambda array: pl.BlockSpec(array.shape, lambda step: (0,) * array.ndim)
    tables = (forward_x, forward_z, back_z, back_x)

    def exchange(block):
        block = block.reshape(count, per_chunk * 2, lanes)
        return lax.all_to_all(block, "slab", 0, 0, tiled=True).reshape(rows, lanes)

    returned = []
    for chunk in range(chunks):
        data = exchange(sent[chunk])
        data = call(
            functools.partial(middle_kernel, count, planes, per_chunk),
            flat,
            grid=(per_chunk,),
            in_specs=[
                pl.BlockSpec((rows, lanes), lambda step: (0, 0)),
                pl.BlockSpec(
                    (1, grid_len, grid_len),
                    functools.partial(lambda first, step: (first + step, 0, 0), chunk * per_chunk),
                ),
            ]
            + [whole(table) for table in tables],
            out_specs=pl.BlockSpec((rows, lanes), lambda step: (0, 0)),
            scratch_shapes=[pltpu.VMEM((pl.cdiv(lanes, 128), rows, 128), jnp.float32)] * 2,
        )(data, gain_zx, *tables)
        returned.append(exchange(data))
    return call(
        functools.partial(gather_kernel, chunks),
        jax.ShapeDtypeStruct(image.shape, jnp.float32),
    )(*returned, coil_map, back_y)


def on_device(image, prox_point, dual, adjoint_data, coil_maps, kernel):
    gain_zx = jnp.transpose(kernel, (0, 2, 1))
    normal = filtered_normal(image, coil_maps[0], gain_zx)
    for coil in range(1, coil_maps.shape[0]):
        normal = normal + filtered_normal(image, coil_maps[coil], gain_zx)
    normal = lax.psum(normal, "coil")
    image_new = image - step_size * (normal - adjoint_data + penalty * (image - prox_point + dual))
    merged = image_new + dual
    extended = extended_2(merged, (("slab", 1),), 1)
    planes = merged.shape[1]
    base = lax.axis_index("slab") * planes
    prox_new = 0.5 * (spin(extended, base, 0) + spin(extended, base, 1))
    dual_new = dual + image_new - prox_new
    return (image_new, prox_new, dual_new)


def solution(mesh):
    in_specs = (
        P("recon", "slab", None, None),
        P("recon", "slab", None, None),
        P("recon", "slab", None, None),
        P("recon", "slab", None, None),
        P("coil", "recon", "slab", None, None),
        P("slab", None, None),
    )
    out_specs = (
        P("recon", "slab", None, None),
        P("recon", "slab", None, None),
        P("recon", "slab", None, None),
    )
    return jax.shard_map(
        on_device, mesh=mesh, in_specs=in_specs, out_specs=out_specs, check_vma=False
    )
```

```python
import functools
import math

import jax
import jax.numpy as jnp
import ml_dtypes
import numpy as np
from jax import lax
from jax.experimental import pallas as pl
from jax.experimental.pallas import tpu as pltpu
from jax.sharding import PartitionSpec as P

half_root = 0.7071067811865476
shrink = 0.5
step_size = 0.25
penalty = 1.0
VMEM_LIMIT = 56 * 1024 * 1024


def real_form(rows, cols, length, direction, gain=1.0):
    angle = 2.0 * math.pi / length * (np.outer(rows, cols) % length).astype(np.float64)
    cosine = np.cos(angle) * gain
    sine = direction * np.sin(angle) * gain
    return np.concatenate(
        [np.concatenate([cosine, sine], 1), np.concatenate([-sine, cosine], 1)], 0
    )


def three_way(table, axis):
    high = table.astype(ml_dtypes.bfloat16)
    low = (table - high.astype(np.float64)).astype(ml_dtypes.bfloat16)
    return np.concatenate([high, high, low], axis)


def split(values):
    high = values.astype(jnp.bfloat16)
    low = (values - high.astype(jnp.float32)).astype(jnp.bfloat16)
    return high, low


def stacked(parts, axis):
    pairs = [split(part) for part in parts]
    highs = [pair[0] for pair in pairs]
    lows = [pair[1] for pair in pairs]
    return jnp.concatenate(highs + lows + highs, axis=axis)


def product(left, right):
    return jnp.dot(left, right, preferred_element_type=jnp.float32)


def coil_image(image_ref, coil_ref, right_ref):
    planes = image_ref.shape[1]
    reals, imags = [], []
    for plane in range(planes):
        img_r, img_i = image_ref[0, plane], image_ref[1, plane]
        map_r, map_i = coil_ref[0, plane], coil_ref[1, plane]
        reals.append(map_r * img_r - map_i * img_i)
        imags.append(map_r * img_i + map_i * img_r)
    right_ref[...] = stacked([jnp.concatenate(reals, axis=1), jnp.concatenate(imags, axis=1)], 0)


def lane_tiles(lanes):
    return [(tile, min(128, lanes - tile * 128)) for tile in range(pl.cdiv(lanes, 128))]


def put_rows(out_ref, count, lines, line, rows):
    pitch = out_ref.shape[0] // count
    for tile, size in lane_tiles(rows.shape[1]):
        cells = rows[:, tile * 128 : tile * 128 + size]
        if size < 128:
            cells = jnp.pad(cells, ((0, 0), (0, 128 - size)))
        out_ref[pl.ds(tile * lines + line, count, stride=pitch), :] = cells


def get_rows(data_ref, count, lines, line, tiles):
    pitch = data_ref.shape[0] // count
    return jnp.concatenate(
        [data_ref[pl.ds(tile * lines + line, count, stride=pitch), :] for tile in tiles], axis=1
    )


def spread(count, lines, right, table_ref, out_ref):
    cells = product(table_ref[...], right)
    for line in range(lines):
        put_rows(out_ref, count, lines, line, cells[line * count : (line + 1) * count])


def spread_first_kernel(count, lines, image_ref, coil_ref, table_ref, out_ref, right_ref):
    coil_image(image_ref, coil_ref, right_ref)
    spread(count, lines, right_ref[...], table_ref, out_ref)


def spread_kernel(count, lines, right_ref, table_ref, out_ref):
    spread(count, lines, right_ref[...], table_ref, out_ref)


def middle_kernel(count, planes, width, lines, data_ref, gain_ref, fx_ref, fz_ref, gz_ref, gx_ref, out_ref):
    step = pl.program_id(0)
    grid_len = gain_ref.shape[1]
    depth = count * planes
    tiles = range(pl.cdiv(planes * width, 128))

    def part_of(part):
        rows = get_rows(data_ref, count, lines, 2 * step + part, tiles)
        return jnp.concatenate(
            [rows[:, plane * width : (plane + 1) * width] for plane in range(planes)], axis=0
        )

    left = stacked([part_of(0), part_of(1)], 1)
    along_x = product(left, fx_ref[...])
    right = stacked([along_x[:, :grid_len], along_x[:, grid_len:]], 0)
    spectrum = product(fz_ref[...], right)
    gain = gain_ref[0]
    right = stacked([spectrum[:grid_len] * gain, spectrum[grid_len:] * gain], 0)
    along_x = product(gz_ref[...], right)
    left = stacked([along_x[:depth], along_x[depth:]], 1)
    cells = product(left, gx_ref[...])
    for part in range(2):
        rows = jnp.concatenate(
            [
                cells[plane * count : (plane + 1) * count, part * width : (part + 1) * width]
                for plane in range(planes)
            ],
            axis=1,
        )
        put_rows(out_ref, count, lines, 2 * step + part, rows)


def lines_back(count, lines, data_ref, table_ref, tiles):
    rows = [get_rows(data_ref, count, lines, line, tiles) for line in range(lines)]
    return product(table_ref[...], stacked([jnp.concatenate(rows, axis=0)], 0))


def back_kernel(count, lines, lanes, data_ref, table_ref, *refs):
    field = lines_back(count, lines, data_ref, table_ref, range(pl.cdiv(lanes, 128)))
    if len(refs) == 2:
        field = field + refs[0][...]
    refs[-1][...] = field


def plane_normal(field, coil_ref, plane, start):
    height, width = coil_ref.shape[-2:]
    real = field[:height, start : start + width]
    imag = field[height:, start : start + width]
    map_r, map_i = coil_ref[0, plane], coil_ref[1, plane]
    return map_r * real + map_i * imag, map_r * imag - map_i * real


def normal_kernel(field_ref, coil_ref, out_ref):
    planes, height, width = coil_ref.shape[1:]
    for plane in range(planes):
        out_ref[0, plane], out_ref[1, plane] = plane_normal(field_ref, coil_ref, plane, plane * width)


def edge_kernel(count, lines, data_ref, table_ref, part_ref, coil_ref, base_ref, dual_ref, low_ref, high_ref):
    planes, height, width = coil_ref.shape[1:]
    for plane, out_ref in ((0, low_ref), (planes - 1, high_ref)):
        first = plane * width // 128
        tiles = range(first, pl.cdiv((plane + 1) * width, 128))
        field = lines_back(count, lines, data_ref, table_ref, tiles)
        field = field + part_ref[:, tiles[0] * 128 : (tiles[-1] + 1) * 128]
        normal = plane_normal(field, coil_ref, plane, plane * width - first * 128)
        for part in range(2):
            image_new = base_ref[part, plane] - step_size * normal[part]
            out_ref[part] = image_new + dual_ref[part, plane]


THRESHOLD = shrink / (half_root**3)


def store_plane(ref, index, part, cells):
    height, width = cells.shape
    ref[index + (part, 0, slice(0, height))] = cells[:, :128]
    tail = jnp.concatenate([cells[:, 128:], cells[:, : 256 - width]], axis=1)
    ref[index + (part, 1, slice(0, height))] = tail
    ref[index + (part, 0, slice(height, height + 8))] = cells[:8, :128]
    ref[index + (part, 1, slice(height, height + 8))] = tail[:8]


def swap_pairs(values, even):
    return jnp.where(
        even, values + pltpu.roll(values, 127, 1), pltpu.roll(values, 1, 1) - values
    )


def spin_rows(offset, width, first, second):
    lane = lax.broadcasted_iota(jnp.int32, (8, 128), 1)
    even = lane % 2 == 0
    coefs = []
    for part in range(2):
        tiles = []
        for tile in range(2):
            a_0, a_1 = first(part, tile, 0), first(part, tile, 1)
            b_0, b_1 = second(part, tile, 0), second(part, tile, 1)
            sum_0, sum_1, dif_0, dif_1 = a_0 + b_0, a_1 + b_1, a_0 - b_0, a_1 - b_1
            tiles.append([sum_0 + sum_1, sum_0 - sum_1, dif_0 + dif_1, dif_0 - dif_1])
        if offset:
            for band in range(4):
                low, high = pltpu.roll(tiles[0][band], 127, 1), pltpu.roll(tiles[1][band], 127, 1)
                tiles[0][band] = jnp.where(lane == 127, high, low)
                tiles[1][band] = high
        coefs.append([[swap_pairs(band, even) for band in bands] for bands in tiles])
    for tile in range(2):
        for band in range(4):
            real, imag = coefs[0][tile][band], coefs[1][tile][band]
            square = jnp.maximum(real * real + imag * imag, THRESHOLD * THRESHOLD)
            factor = 1.0 - THRESHOLD * lax.rsqrt(square)
            if band == 0:
                factor = jnp.where(even, 1.0, factor)
            coefs[0][tile][band] = swap_pairs(real * factor, even)
            coefs[1][tile][band] = swap_pairs(imag * factor, even)
    scale = 0.5 * half_root**6
    spun = []
    for part in range(2):
        tiles = []
        for tile in range(2):
            bands = [band * scale for band in coefs[part][tile]]
            sum_0, sum_1 = bands[0] + bands[1], bands[0] - bands[1]
            dif_0, dif_1 = bands[2] + bands[3], bands[2] - bands[3]
            tiles.append([[sum_0 + dif_0, sum_1 + dif_1], [sum_0 - dif_0, sum_1 - dif_1]])
        if offset:
            for plane in range(2):
                for which in range(2):
                    low, high = tiles[0][plane][which], tiles[1][plane][which]
                    wrapped = pltpu.roll(high, 128 - (width - 129), 1)
                    tiles[1][plane][which] = jnp.where(
                        lane == 0, pltpu.roll(low, 1, 1), pltpu.roll(high, 1, 1)
                    )
                    tiles[0][plane][which] = jnp.where(lane == 0, wrapped, pltpu.roll(low, 1, 1))
        spun.append(tiles)
    return spun


def spin_pair(offset, height, width, load_first, load_second, store):
    def body(group, _):
        def rows_of(which):
            return pl.ds(group * 16 + offset + which, 8, stride=2)

        spun = spin_rows(
            offset,
            width,
            lambda part, tile, which: load_first(part, tile, rows_of(which)),
            lambda part, tile, which: load_second(part, tile, rows_of(which)),
        )
        for part in range(2):
            for tile in range(2):
                for plane in range(2):
                    for which in range(2):
                        store(plane, part, tile, rows_of(which), spun[part][tile][plane][which])
        return 0

    lax.fori_loop(0, height // 16, body, 0)


def finish_kernel(
    count, lines, data_ref, table_ref, part_ref, coil_ref, base_ref, dual_ref,
    image_ref, prox_ref, dual_out_ref, merged, total,
):
    planes, height, width = coil_ref.shape[1:]
    tiles = range(pl.cdiv(planes * width, 128))
    field = lines_back(count, lines, data_ref, table_ref, tiles) + part_ref[...]
    for plane in range(planes):
        normal = plane_normal(field, coil_ref, plane, plane * width)
        for part in range(2):
            image_new = base_ref[part, plane] - step_size * normal[part]
            image_ref[part, plane] = image_new
            store_plane(merged, (plane,), part, image_new + dual_ref[part, plane])

    def loader(plane):
        return lambda part, tile, rows: merged[plane, part, tile, rows, :]

    for low in range(0, planes, 2):

        def store(plane, part, tile, rows, cells, low=low):
            total[low + plane, part, tile, rows, :] = cells

        spin_pair(0, height, width, loader(low), loader(low + 1), store)
    total[:, :, :, height:, :] = jnp.zeros((planes, 2, 2, 8, 128), jnp.float32)
    for low in range(1, planes - 1, 2):

        def store(plane, part, tile, rows, cells, low=low):
            total[low + plane, part, tile, rows, :] += cells

        spin_pair(1, height, width, loader(low), loader(low + 1), store)
    for plane in range(planes):
        for part in range(2):
            for tile, size in ((0, 128), (1, width - 128)):
                lanes = slice(tile * 128, tile * 128 + size)
                total[plane, part, tile, :8, :] += total[plane, part, tile, height:, :]
                prox = total[plane, part, tile, :height, :size]
                prox_ref[part, plane, :, lanes] = prox
                dual_out_ref[part, plane, :, lanes] = merged[plane, part, tile, :height, :size] - prox


def rim_kernel(low_ref, high_ref, before_ref, after_ref, prox_ref, dual_ref, prox_out, dual_out, planes, total):
    height, width = low_ref.shape[-2:]
    is_low = pl.program_id(0) == 0
    for part in range(2):
        store_plane(planes, (0,), part, jnp.where(is_low, before_ref[part], high_ref[part]))
        store_plane(planes, (1,), part, jnp.where(is_low, low_ref[part], after_ref[part]))
    total[:, :, height:, :] = jnp.zeros((2, 2, 8, 128), jnp.float32)

    def loader(plane):
        return lambda part, tile, rows: planes[plane, part, tile, rows, :]

    kept = []

    def store(plane, part, tile, rows, cells):
        if plane == 0:
            kept.append(cells)
            return
        total[part, tile, rows, :] = jnp.where(is_low, cells, kept.pop(0))

    spin_pair(1, height, width, loader(0), loader(1), store)
    for part in range(2):
        for tile, size in ((0, 128), (1, width - 128)):
            lanes = slice(tile * 128, tile * 128 + size)
            total[part, tile, :1, :] = total[part, tile, height : height + 1, :]
            cells = total[part, tile, :height, :size]
            prox_out[part, 0, :, lanes] = prox_ref[part, 0, :, lanes] + cells
            dual_out[part, 0, :, lanes] = dual_ref[part, 0, :, lanes] - cells


def call(kernel, out_shape, micros, **extra):
    return pl.pallas_call(
        kernel,
        out_shape=out_shape,
        cost_estimate=pl.CostEstimate(
            flops=int(micros * 1e9), bytes_accessed=int(micros * 1e6), transcendentals=0
        ),
        compiler_params=pltpu.CompilerParams(vmem_limit_bytes=VMEM_LIMIT),
        **extra,
    )


def extended_2(cells, sides, width):
    for axis, dim in sides:
        count = lax.axis_size(axis)
        head = lax.slice_in_dim(cells, 0, width, axis=dim)
        tail = lax.slice_in_dim(cells, cells.shape[dim] - width, cells.shape[dim], axis=dim)
        cells = jnp.concatenate(
            [
                lax.ppermute(tail, axis, [(i, (i + 1) % count) for i in range(count)]),
                cells,
                lax.ppermute(head, axis, [((i + 1) % count, i) for i in range(count)]),
            ],
            axis=dim,
        )
    return cells


def pair_local(values, axis_dim, offset):
    length = values.shape[axis_dim]
    layout = [1] * values.ndim
    layout[axis_dim] = length
    is_first = ((jnp.arange(length) - offset) % 2 == 0).reshape(layout)
    after_one = jnp.roll(values, -1, axis_dim)
    before_one = jnp.roll(values, 1, axis_dim)
    return jnp.where(is_first, (values + after_one) * half_root, (before_one - values) * half_root)


def pair_planes(extended, own_first):
    middle = extended[:, 1:-1]
    after_one = extended[:, 2:]
    before_one = extended[:, :-2]
    marked = own_first[None, :, None, None]
    return jnp.where(marked, (middle + after_one) * half_root, (before_one - middle) * half_root)


def spin(extended, base, offset):
    total_planes = extended.shape[1]
    global_plane = base - 1 + jnp.arange(total_planes, dtype=jnp.int32)
    plane_first = (global_plane - offset) % 2 == 0
    own_first = plane_first[1:-1]
    lower_rim = (extended[:, :1] + extended[:, 1:2]) * half_root
    upper_rim = (extended[:, -2:-1] - extended[:, -1:]) * half_root
    coefs = jnp.concatenate([lower_rim, pair_planes(extended, own_first), upper_rim], axis=1)
    coefs = pair_local(coefs, 2, offset)
    coefs = pair_local(coefs, 3, offset)
    rows_first = (jnp.arange(extended.shape[2]) - offset) % 2 == 0
    cols_first = (jnp.arange(extended.shape[3]) - offset) % 2 == 0
    keep = plane_first[:, None, None] & rows_first[None, :, None] & cols_first[None, None, :]
    magnitude = jnp.sqrt(coefs[0] * coefs[0] + coefs[1] * coefs[1])
    factor = jnp.maximum(magnitude - shrink, 0.0) / jnp.maximum(magnitude, shrink)
    coefs = jnp.where(keep[None], coefs, coefs * factor[None])
    coefs = pair_local(coefs, 3, offset)
    coefs = pair_local(coefs, 2, offset)
    return pair_planes(coefs, own_first)


class Plan:
    def __init__(self, shape, lines, grid_len):
        self.count = count = lax.axis_size("slab")
        self.grid_len = grid_len
        _, self.planes, self.height, self.width = shape
        depth = count * self.planes
        self.chunks = chunks = 2 if lines % 2 == 0 else 1
        self.per_chunk = per_chunk = lines // chunks
        self.lines = per_chunk * 2
        self.lanes = self.planes * self.width
        self.padded = pl.cdiv(self.lanes, 128) * 128
        self.pitch = pl.cdiv(self.padded // 128 * self.lines, 8) * 8
        freq = np.arange(grid_len)

        def y_order(table, axis):
            order = np.arange(2 * grid_len).reshape(2, count, chunks, per_chunk)
            order = order.transpose(2, 3, 0, 1).reshape(chunks, -1)
            return [np.take(table, part, axis) for part in order]

        forward = real_form(np.arange(self.height), freq, grid_len, -1.0).T
        self.forward_y = [three_way(part, 1) for part in y_order(forward, 0)]
        back = real_form(freq, np.arange(self.height), grid_len, 1.0, 1.0 / grid_len).T
        self.back_y = [three_way(part, 1) for part in y_order(back, 1)]
        z_order = np.arange(depth).reshape(count, self.planes).T.reshape(depth)
        self.middle = (
            three_way(real_form(np.arange(self.width), freq, grid_len, -1.0), 0),
            three_way(real_form(z_order, freq, grid_len, -1.0).T, 1),
            three_way(real_form(freq, z_order, grid_len, 1.0, 1.0 / grid_len).T, 1),
            three_way(real_form(freq, np.arange(self.width), grid_len, 1.0, 1.0 / grid_len), 0),
        )


def returned_lines(plan, image, coil_map, gain_zx):
    count, lines = plan.count, plan.lines
    buffer = jax.ShapeDtypeStruct((count * plan.pitch, 128), jnp.float32)
    right = jax.ShapeDtypeStruct((6 * plan.height, plan.lanes), jnp.bfloat16)
    first, right = call(
        functools.partial(spread_first_kernel, count, lines), [buffer, right], 5
    )(image, coil_map, plan.forward_y[0])
    sent = [first]
    for chunk in range(1, plan.chunks):
        sent.append(
            call(functools.partial(spread_kernel, count, lines), buffer, 3)(
                right, plan.forward_y[chunk]
            )
        )

    def exchange(block):
        block = block.reshape(count, plan.pitch, 128)
        return lax.all_to_all(block, "slab", 0, 0, tiled=True).reshape(buffer.shape)

    whole = lambda array: pl.BlockSpec(array.shape, lambda step: (0,) * array.ndim)
    returned = []
    for chunk in range(plan.chunks):
        data = exchange(sent[chunk])
        at = functools.partial(lambda first, step: (first + step, 0, 0), chunk * plan.per_chunk)
        data = call(
            functools.partial(middle_kernel, count, plan.planes, plan.width, lines),
            buffer,
            5 * plan.per_chunk,
            grid=(plan.per_chunk,),
            in_specs=[whole(buffer), pl.BlockSpec((1,) + gain_zx.shape[1:], at)]
            + [whole(table) for table in plan.middle],
            out_specs=whole(buffer),
        )(data, gain_zx, *plan.middle)
        returned.append(exchange(data))
    return returned


def partial_field(plan, returned):
    field = jax.ShapeDtypeStruct((2 * plan.height, plan.padded), jnp.float32)
    total = ()
    for chunk, data in enumerate(returned):
        kernel = functools.partial(back_kernel, plan.count, plan.lines, plan.lanes)
        total = (call(kernel, field, 4)(data, plan.back_y[chunk], *total),)
    return total[0]


def neighbours(low, high):
    count = lax.axis_size("slab")
    before = lax.ppermute(high, "slab", [(i, (i + 1) % count) for i in range(count)])
    after = lax.ppermute(low, "slab", [((i + 1) % count, i) for i in range(count)])
    return before, after


def finish(plan, returned, coil_map, base, dual):
    planes, height, width = plan.planes, plan.height, plan.width
    part = partial_field(plan, returned[:-1])
    operands = (returned[-1], plan.back_y[-1], part, coil_map, base, dual)
    sizes = (plan.count, plan.lines)
    plane = jax.ShapeDtypeStruct((2, height, width), jnp.float32)
    low, high = call(functools.partial(edge_kernel, *sizes), [plane] * 2, 3)(*operands)
    before, after = neighbours(low, high)
    field = jax.ShapeDtypeStruct(dual.shape, jnp.float32)
    scratch = pltpu.VMEM((planes, 2, 2, height + 8, 128), jnp.float32)
    image_new, prox, dual_new = call(
        functools.partial(finish_kernel, *sizes), [field] * 3, 12, scratch_shapes=[scratch] * 2
    )(*operands)
    own = pl.BlockSpec((2, 1, height, width), lambda step: (0, step * (planes - 1), 0, 0))
    whole = pl.BlockSpec(plane.shape, lambda step: (0, 0, 0))
    prox, dual_new = call(
        rim_kernel,
        [field] * 2,
        3,
        grid=(2,),
        in_specs=[whole] * 4 + [own] * 2,
        out_specs=[own] * 2,
        input_output_aliases={4: 0, 5: 1},
        scratch_shapes=[
            pltpu.VMEM((2, 2, 2, height + 8, 128), jnp.float32),
            pltpu.VMEM((2, 2, height + 8, 128), jnp.float32),
        ],
    )(low, high, before, after, prox, dual_new)
    return image_new, prox, dual_new


def on_device(image, prox_point, dual, adjoint_data, coil_maps, kernel):
    plan = Plan(image.shape, *kernel.shape[:2])
    gain_zx = jnp.transpose(kernel, (0, 2, 1))
    base = image + step_size * (adjoint_data - penalty * (image - prox_point + dual))
    coils = coil_maps.shape[0]
    returned = [returned_lines(plan, image, coil_maps[coil], gain_zx) for coil in range(coils)]
    alone = coils * lax.axis_size("coil") == 1
    if alone and plan.planes % 2 == 0 and plan.height % 16 == 0 and 128 < plan.width < 256:
        return finish(plan, returned[0], coil_maps[0], base, dual)
    normal = jnp.zeros_like(image)
    for coil in range(coils):
        field = partial_field(plan, returned[coil])
        normal = normal + call(
            normal_kernel, jax.ShapeDtypeStruct(image.shape, jnp.float32), 3
        )(field, coil_maps[coil])
    normal = lax.psum(normal, "coil")
    image_new = base - step_size * normal
    merged = image_new + dual
    extended = extended_2(merged, (("slab", 1),), 1)
    first = lax.axis_index("slab") * plan.planes
    prox_new = 0.5 * (spin(extended, first, 0) + spin(extended, first, 1))
    return (image_new, prox_new, merged - prox_new)


def solution(mesh):
    in_specs = (
        P("recon", "slab", None, None),
        P("recon", "slab", None, None),
        P("recon", "slab", None, None),
        P("recon", "slab", None, None),
        P("coil", "recon", "slab", None, None),
        P("slab", None, None),
    )
    out_specs = (
        P("recon", "slab", None, None),
        P("recon", "slab", None, None),
        P("recon", "slab", None, None),
    )
    return jax.shard_map(
        on_device, mesh=mesh, in_specs=in_specs, out_specs=out_specs, check_vma=False
    )
```

```python
import functools
import math

import jax
import jax.numpy as jnp
import ml_dtypes
import numpy as np
from jax import lax
from jax.experimental import pallas as pl
from jax.experimental.pallas import tpu as pltpu
from jax.sharding import PartitionSpec as P

half_root = 0.7071067811865476
shrink = 0.5
step_size = 0.25
penalty = 1.0
EPI = 28


def real_form(rows, cols, length, direction, gain=1.0):
    angle = 2.0 * math.pi / length * (np.outer(rows, cols) % length).astype(np.float64)
    cosine = np.cos(angle) * gain
    sine = direction * np.sin(angle) * gain
    return np.concatenate(
        [np.concatenate([cosine, sine], 1), np.concatenate([-sine, cosine], 1)], 0
    )


def three_way(table, axis):
    high = table.astype(ml_dtypes.bfloat16)
    low = (table - high.astype(np.float64)).astype(ml_dtypes.bfloat16)
    return np.concatenate([high, high, low], axis)


def split(values):
    high = values.astype(jnp.bfloat16)
    low = (values - high.astype(jnp.float32)).astype(jnp.bfloat16)
    return high, low


def stacked(parts, axis):
    pairs = [split(part) for part in parts]
    highs = [pair[0] for pair in pairs]
    lows = [pair[1] for pair in pairs]
    return jnp.concatenate(highs + lows + highs, axis=axis)


def product(left, right):
    return jnp.dot(left, right, preferred_element_type=jnp.float32)


def coil_image(image_ref, coil_ref, right_ref):
    planes = image_ref.shape[1]
    reals, imags = [], []
    for plane in range(planes):
        img_r, img_i = image_ref[0, plane], image_ref[1, plane]
        map_r, map_i = coil_ref[0, plane], coil_ref[1, plane]
        reals.append(map_r * img_r - map_i * img_i)
        imags.append(map_r * img_i + map_i * img_r)
    right_ref[...] = stacked([jnp.concatenate(reals, axis=1), jnp.concatenate(imags, axis=1)], 0)


def lane_tiles(lanes):
    return [(tile, min(128, lanes - tile * 128)) for tile in range(pl.cdiv(lanes, 128))]


def put_rows(out_ref, count, lines, line, rows):
    pitch = out_ref.shape[0] // count
    for tile, size in lane_tiles(rows.shape[1]):
        cells = rows[:, tile * 128 : tile * 128 + size]
        if size < 128:
            cells = jnp.pad(cells, ((0, 0), (0, 128 - size)))
        out_ref[pl.ds(tile * lines + line, count, stride=pitch), :] = cells


def get_rows(data_ref, count, lines, line, tiles):
    pitch = data_ref.shape[0] // count
    return jnp.concatenate(
        [data_ref[pl.ds(tile * lines + line, count, stride=pitch), :] for tile in tiles], axis=1
    )


def spread(count, lines, right, table_ref, out_ref):
    cells = product(table_ref[...], right)
    for line in range(lines):
        put_rows(out_ref, count, lines, line, cells[line * count : (line + 1) * count])


def spread_first_kernel(count, lines, image_ref, coil_ref, table_ref, out_ref, right_ref):
    coil_image(image_ref, coil_ref, right_ref)
    spread(count, lines, right_ref[...], table_ref, out_ref)


def spread_kernel(count, lines, right_ref, table_ref, out_ref):
    spread(count, lines, right_ref[...], table_ref, out_ref)


def middle_kernel(count, planes, width, lines, data_ref, gain_ref, fx_ref, fz_ref, gz_ref, gx_ref, out_ref):
    step = pl.program_id(0)
    grid_len = gain_ref.shape[1]
    depth = count * planes
    tiles = range(pl.cdiv(planes * width, 128))

    def part_of(part):
        rows = get_rows(data_ref, count, lines, 2 * step + part, tiles)
        return jnp.concatenate(
            [rows[:, plane * width : (plane + 1) * width] for plane in range(planes)], axis=0
        )

    left = stacked([part_of(0), part_of(1)], 1)
    along_x = product(left, fx_ref[...])
    right = stacked([along_x[:, :grid_len], along_x[:, grid_len:]], 0)
    spectrum = product(fz_ref[...], right)
    gain = gain_ref[0]
    right = stacked([spectrum[:grid_len] * gain, spectrum[grid_len:] * gain], 0)
    along_x = product(gz_ref[...], right)
    left = stacked([along_x[:depth], along_x[depth:]], 1)
    cells = product(left, gx_ref[...])
    for part in range(2):
        rows = jnp.concatenate(
            [
                cells[plane * count : (plane + 1) * count, part * width : (part + 1) * width]
                for plane in range(planes)
            ],
            axis=1,
        )
        put_rows(out_ref, count, lines, 2 * step + part, rows)


def lines_back(count, lines, data_ref, table_ref, tiles):
    rows = [get_rows(data_ref, count, lines, line, tiles) for line in range(lines)]
    return product(table_ref[...], stacked([jnp.concatenate(rows, axis=0)], 0))


def back_kernel(count, lines, lanes, data_ref, table_ref, *refs):
    field = lines_back(count, lines, data_ref, table_ref, range(pl.cdiv(lanes, 128)))
    if len(refs) == 2:
        field = field + refs[0][...]
    refs[-1][...] = field


def plane_normal(field, coil_ref, plane, start):
    height, width = coil_ref.shape[-2:]
    real = field[:height, start : start + width]
    imag = field[height:, start : start + width]
    map_r, map_i = coil_ref[0, plane], coil_ref[1, plane]
    return map_r * real + map_i * imag, map_r * imag - map_i * real


def normal_kernel(field_ref, coil_ref, out_ref):
    planes, height, width = coil_ref.shape[1:]
    for plane in range(planes):
        out_ref[0, plane], out_ref[1, plane] = plane_normal(field_ref, coil_ref, plane, plane * width)


def update_kernel(
    count, lines, data_ref, table_ref, part_ref, coil_ref, base_ref, dual_ref,
    image_ref, merged_ref, low_ref, high_ref,
):
    planes, height, width = coil_ref.shape[1:]
    tiles = range(pl.cdiv(planes * width, 128))
    field = lines_back(count, lines, data_ref, table_ref, tiles) + part_ref[...]
    for plane in range(planes):
        normal = plane_normal(field, coil_ref, plane, plane * width)
        for part in range(2):
            image_new = base_ref[part, plane] - step_size * normal[part]
            merged = image_new + dual_ref[part, plane]
            image_ref[part, plane] = image_new
            merged_ref[part, plane] = merged
            if plane == 0:
                low_ref[part] = merged
            if plane == planes - 1:
                high_ref[part] = merged


THRESHOLD = shrink / (half_root**3)


def pairing(width, offset):
    table = np.zeros((width, 256))
    for pair in range(width // 2):
        first, second = (2 * pair + offset) % width, (2 * pair + 1 + offset) % width
        table[first, pair] = table[second, pair] = table[first, 128 + pair] = 1.0
        table[second, 128 + pair] = -1.0
    return table


def pairing_tables(width, offset):
    table = pairing(width, offset)
    padded = np.concatenate([table, np.zeros((256 - width, 256))], 0)
    to_pairs = np.concatenate([padded, padded], 0).astype(ml_dtypes.bfloat16)
    back = np.concatenate([table.T, table.T], 0).astype(ml_dtypes.bfloat16)
    return to_pairs, back


def pair_lanes(cells, table_ref, band_ref, index):
    height, width = cells.shape
    high, low = split(jnp.pad(cells, ((0, 0), (0, 256 - width))))
    bands = product(jnp.concatenate([high, low], axis=1), table_ref[...])
    for tile in range(2):
        band = bands[:, tile * 128 : tile * 128 + 128]
        band_ref[index + (tile, slice(0, height))] = band
        band_ref[index + (tile, slice(height, height + 8))] = band[:8]


def unpair_lanes(table_ref, band_ref, index, height):
    parts = [split(band_ref[index + (tile, slice(0, height))]) for tile in range(2)]
    left = [part[0] for part in parts] + [part[1] for part in parts]
    return product(jnp.concatenate(left, axis=1), table_ref[...])


def shrink_planes(offset, height, band_ref, first, second):
    scale = 0.5 * half_root**6
    refs = (first, second)

    def body(group, _):
        picks = [pl.ds(group * 16 + offset + which, 8, stride=2) for which in range(2)]
        for tile in range(2):
            coefs = []
            for part in range(2):
                (a_0, a_1), (b_0, b_1) = (
                    [band_ref[plane, part, tile, pick, :] for pick in picks] for plane in refs
                )
                sum_0, sum_1, dif_0, dif_1 = a_0 + b_0, a_1 + b_1, a_0 - b_0, a_1 - b_1
                coefs.append([sum_0 + sum_1, sum_0 - sum_1, dif_0 + dif_1, dif_0 - dif_1])
            for band in range(4):
                real, imag = coefs[0][band], coefs[1][band]
                if band == 0 and tile == 0:
                    factor = scale
                else:
                    square = jnp.maximum(real * real + imag * imag, THRESHOLD * THRESHOLD)
                    factor = scale - (scale * THRESHOLD) * lax.rsqrt(square)
                coefs[0][band], coefs[1][band] = real * factor, imag * factor
            for part in range(2):
                bands = coefs[part]
                sum_0, sum_1 = bands[0] + bands[1], bands[0] - bands[1]
                dif_0, dif_1 = bands[2] + bands[3], bands[2] - bands[3]
                spun = ((sum_0 + dif_0, sum_1 + dif_1), (sum_0 - dif_0, sum_1 - dif_1))
                for plane, rows in zip(refs, spun):
                    for pick, row in zip(picks, rows):
                        band_ref[plane, part, tile, pick, :] = row
        return 0

    lax.fori_loop(0, height // 16, body, 0, unroll=2)


def spin_0_kernel(merged_ref, to_ref, back_ref, out_ref, bands):
    _, planes, height, _ = merged_ref.shape
    for low in range(0, planes, 2):
        for plane in (low, low + 1):
            for part in range(2):
                pair_lanes(merged_ref[part, plane], to_ref, bands, (plane, part))
        shrink_planes(0, height, bands, low, low + 1)
        for plane in (low, low + 1):
            for part in range(2):
                out_ref[part, plane] = unpair_lanes(back_ref, bands, (plane, part), height)


def spin_1_kernel(merged_ref, before_ref, after_ref, half_ref, to_ref, back_ref, prox_ref, dual_ref, bands):
    _, planes, height, _ = merged_ref.shape

    def cells_of(plane, part):
        if plane < 0:
            return before_ref[part]
        return after_ref[part] if plane == planes else merged_ref[part, plane]

    for low in range(-1, planes, 2):
        for plane in (low, low + 1):
            for part in range(2):
                pair_lanes(cells_of(plane, part), to_ref, bands, (plane + 1, part))
        shrink_planes(1, height, bands, low + 1, low + 2)
        for plane in (low, low + 1):
            if 0 <= plane < planes:
                for part in range(2):
                    for tile in range(2):
                        at = (plane + 1, part, tile)
                        bands[at + (slice(0, 1),)] = bands[at + (slice(height, height + 1),)]
                    spun = unpair_lanes(back_ref, bands, (plane + 1, part), height)
                    prox = half_ref[part, plane] + spun
                    prox_ref[part, plane] = prox
                    dual_ref[part, plane] = merged_ref[part, plane] - prox


def call(kernel, out_shape, micros, vmem=56, **extra):
    return pl.pallas_call(
        kernel,
        out_shape=out_shape,
        cost_estimate=pl.CostEstimate(
            flops=int(micros * 1e9), bytes_accessed=int(micros * 1e6), transcendentals=0
        ),
        compiler_params=pltpu.CompilerParams(vmem_limit_bytes=vmem * 1024 * 1024),
        **extra,
    )


def extended_2(cells, sides, width):
    for axis, dim in sides:
        count = lax.axis_size(axis)
        head = lax.slice_in_dim(cells, 0, width, axis=dim)
        tail = lax.slice_in_dim(cells, cells.shape[dim] - width, cells.shape[dim], axis=dim)
        cells = jnp.concatenate(
            [
                lax.ppermute(tail, axis, [(i, (i + 1) % count) for i in range(count)]),
                cells,
                lax.ppermute(head, axis, [((i + 1) % count, i) for i in range(count)]),
            ],
            axis=dim,
        )
    return cells


def pair_local(values, axis_dim, offset):
    length = values.shape[axis_dim]
    layout = [1] * values.ndim
    layout[axis_dim] = length
    is_first = ((jnp.arange(length) - offset) % 2 == 0).reshape(layout)
    after_one = jnp.roll(values, -1, axis_dim)
    before_one = jnp.roll(values, 1, axis_dim)
    return jnp.where(is_first, (values + after_one) * half_root, (before_one - values) * half_root)


def pair_planes(extended, own_first):
    middle = extended[:, 1:-1]
    after_one = extended[:, 2:]
    before_one = extended[:, :-2]
    marked = own_first[None, :, None, None]
    return jnp.where(marked, (middle + after_one) * half_root, (before_one - middle) * half_root)


def spin(extended, base, offset):
    total_planes = extended.shape[1]
    global_plane = base - 1 + jnp.arange(total_planes, dtype=jnp.int32)
    plane_first = (global_plane - offset) % 2 == 0
    own_first = plane_first[1:-1]
    lower_rim = (extended[:, :1] + extended[:, 1:2]) * half_root
    upper_rim = (extended[:, -2:-1] - extended[:, -1:]) * half_root
    coefs = jnp.concatenate([lower_rim, pair_planes(extended, own_first), upper_rim], axis=1)
    coefs = pair_local(coefs, 2, offset)
    coefs = pair_local(coefs, 3, offset)
    rows_first = (jnp.arange(extended.shape[2]) - offset) % 2 == 0
    cols_first = (jnp.arange(extended.shape[3]) - offset) % 2 == 0
    keep = plane_first[:, None, None] & rows_first[None, :, None] & cols_first[None, None, :]
    magnitude = jnp.sqrt(coefs[0] * coefs[0] + coefs[1] * coefs[1])
    factor = jnp.maximum(magnitude - shrink, 0.0) / jnp.maximum(magnitude, shrink)
    coefs = jnp.where(keep[None], coefs, coefs * factor[None])
    coefs = pair_local(coefs, 3, offset)
    coefs = pair_local(coefs, 2, offset)
    return pair_planes(coefs, own_first)


class Plan:
    def __init__(self, shape, lines, grid_len):
        self.count = count = lax.axis_size("slab")
        self.grid_len = grid_len
        _, self.planes, self.height, self.width = shape
        depth = count * self.planes
        self.chunks = chunks = 2 if lines % 2 == 0 else 1
        self.per_chunk = per_chunk = lines // chunks
        self.lines = per_chunk * 2
        self.lanes = self.planes * self.width
        self.padded = pl.cdiv(self.lanes, 128) * 128
        self.pitch = pl.cdiv(self.padded // 128 * self.lines, 8) * 8
        freq = np.arange(grid_len)

        def y_order(table, axis):
            order = np.arange(2 * grid_len).reshape(2, count, chunks, per_chunk)
            order = order.transpose(2, 3, 0, 1).reshape(chunks, -1)
            return [np.take(table, part, axis) for part in order]

        forward = real_form(np.arange(self.height), freq, grid_len, -1.0).T
        self.forward_y = [three_way(part, 1) for part in y_order(forward, 0)]
        back = real_form(freq, np.arange(self.height), grid_len, 1.0, 1.0 / grid_len).T
        self.back_y = [three_way(part, 1) for part in y_order(back, 1)]
        z_order = np.arange(depth).reshape(count, self.planes).T.reshape(depth)
        self.middle = (
            three_way(real_form(np.arange(self.width), freq, grid_len, -1.0), 0),
            three_way(real_form(z_order, freq, grid_len, -1.0).T, 1),
            three_way(real_form(freq, z_order, grid_len, 1.0, 1.0 / grid_len).T, 1),
            three_way(real_form(freq, np.arange(self.width), grid_len, 1.0, 1.0 / grid_len), 0),
        )


def returned_lines(plan, image, coil_map, gain_zx):
    count, lines = plan.count, plan.lines
    buffer = jax.ShapeDtypeStruct((count * plan.pitch, 128), jnp.float32)
    right = jax.ShapeDtypeStruct((6 * plan.height, plan.lanes), jnp.bfloat16)
    first, right = call(
        functools.partial(spread_first_kernel, count, lines), [buffer, right], 5
    )(image, coil_map, plan.forward_y[0])
    sent = [first]
    for chunk in range(1, plan.chunks):
        sent.append(
            call(functools.partial(spread_kernel, count, lines), buffer, 3)(
                right, plan.forward_y[chunk]
            )
        )

    def exchange(block):
        block = block.reshape(count, plan.pitch, 128)
        return lax.all_to_all(block, "slab", 0, 0, tiled=True).reshape(buffer.shape)

    whole = lambda array: pl.BlockSpec(array.shape, lambda step: (0,) * array.ndim)
    returned = []
    for chunk in range(plan.chunks):
        data = exchange(sent[chunk])
        at = functools.partial(lambda first, step: (first + step, 0, 0), chunk * plan.per_chunk)
        data = call(
            functools.partial(middle_kernel, count, plan.planes, plan.width, lines),
            buffer,
            5 * plan.per_chunk,
            grid=(plan.per_chunk,),
            in_specs=[whole(buffer), pl.BlockSpec((1,) + gain_zx.shape[1:], at)]
            + [whole(table) for table in plan.middle],
            out_specs=whole(buffer),
        )(data, gain_zx, *plan.middle)
        returned.append(exchange(data))
    return returned


def partial_field(plan, returned):
    field = jax.ShapeDtypeStruct((2 * plan.height, plan.padded), jnp.float32)
    total = ()
    for chunk, data in enumerate(returned):
        kernel = functools.partial(back_kernel, plan.count, plan.lines, plan.lanes)
        total = (call(kernel, field, 4)(data, plan.back_y[chunk], *total),)
    return total[0]


def neighbours(low, high):
    count = lax.axis_size("slab")
    before = lax.ppermute(high, "slab", [(i, (i + 1) % count) for i in range(count)])
    after = lax.ppermute(low, "slab", [((i + 1) % count, i) for i in range(count)])
    return before, after


def finish(plan, returned, coil_map, base, dual):
    planes, height, width = plan.planes, plan.height, plan.width
    part = partial_field(plan, returned[:-1])
    plane = jax.ShapeDtypeStruct((2, height, width), jnp.float32)
    field = jax.ShapeDtypeStruct(dual.shape, jnp.float32)
    image_new, merged, low, high = call(
        functools.partial(update_kernel, plan.count, plan.lines), [field] * 2 + [plane] * 2, 8, EPI
    )(returned[-1], plan.back_y[-1], part, coil_map, base, dual)
    before, after = neighbours(low, high)
    bands = lambda held: [pltpu.VMEM((held, 2, 2, height + 8, 128), jnp.float32)]
    half = call(spin_0_kernel, field, 5, EPI, scratch_shapes=bands(planes))(
        merged, *pairing_tables(width, 0)
    )
    prox, dual_new = call(spin_1_kernel, [field] * 2, 6, EPI, scratch_shapes=bands(planes + 2))(
        merged, before, after, half, *pairing_tables(width, 1)
    )
    return image_new, prox, dual_new


def on_device(image, prox_point, dual, adjoint_data, coil_maps, kernel):
    plan = Plan(image.shape, *kernel.shape[:2])
    gain_zx = jnp.transpose(kernel, (0, 2, 1))
    base = image + step_size * (adjoint_data - penalty * (image - prox_point + dual))
    coils = coil_maps.shape[0]
    returned = [returned_lines(plan, image, coil_maps[coil], gain_zx) for coil in range(coils)]
    alone = coils * lax.axis_size("coil") == 1
    if alone and plan.planes % 2 == 0 and plan.height % 16 == 0 and 128 < plan.width < 256:
        return finish(plan, returned[0], coil_maps[0], base, dual)
    normal = jnp.zeros_like(image)
    for coil in range(coils):
        field = partial_field(plan, returned[coil])
        normal = normal + call(
            normal_kernel, jax.ShapeDtypeStruct(image.shape, jnp.float32), 3
        )(field, coil_maps[coil])
    normal = lax.psum(normal, "coil")
    image_new = base - step_size * normal
    merged = image_new + dual
    extended = extended_2(merged, (("slab", 1),), 1)
    first = lax.axis_index("slab") * plan.planes
    prox_new = 0.5 * (spin(extended, first, 0) + spin(extended, first, 1))
    return (image_new, prox_new, merged - prox_new)


def solution(mesh):
    in_specs = (
        P("recon", "slab", None, None),
        P("recon", "slab", None, None),
        P("recon", "slab", None, None),
        P("recon", "slab", None, None),
        P("coil", "recon", "slab", None, None),
        P("slab", None, None),
    )
    out_specs = (
        P("recon", "slab", None, None),
        P("recon", "slab", None, None),
        P("recon", "slab", None, None),
    )
    return jax.shard_map(
        on_device, mesh=mesh, in_specs=in_specs, out_specs=out_specs, check_vma=False
    )
```

```python
import functools
import math

import jax
import jax.numpy as jnp
import ml_dtypes
import numpy as np
from jax import lax
from jax.experimental import pallas as pl
from jax.experimental.pallas import tpu as pltpu
from jax.sharding import PartitionSpec as P

half_root = 0.7071067811865476
shrink = 0.5
step_size = 0.25
penalty = 1.0
SMALL = 28


def real_form(rows, cols, length, direction, gain=1.0):
    angle = 2.0 * math.pi / length * (np.outer(rows, cols) % length).astype(np.float64)
    cosine = np.cos(angle) * gain
    sine = direction * np.sin(angle) * gain
    return np.concatenate(
        [np.concatenate([cosine, sine], 1), np.concatenate([-sine, cosine], 1)], 0
    )


def three_way(table, axis):
    high = table.astype(ml_dtypes.bfloat16)
    low = (table - high.astype(np.float64)).astype(ml_dtypes.bfloat16)
    return np.concatenate([high, high, low], axis)


def split(values):
    high = values.astype(jnp.bfloat16)
    low = (values - high.astype(jnp.float32)).astype(jnp.bfloat16)
    return high, low


def stacked(parts, axis):
    pairs = [split(part) for part in parts]
    highs = [pair[0] for pair in pairs]
    lows = [pair[1] for pair in pairs]
    return jnp.concatenate(highs + lows + highs, axis=axis)


def product(left, right):
    return jnp.dot(left, right, preferred_element_type=jnp.float32)


def lane_tiles(lanes):
    return [(tile, min(128, lanes - tile * 128)) for tile in range(pl.cdiv(lanes, 128))]


def put_rows(out_ref, count, lines, line, rows, skipped=0):
    pitch = out_ref.shape[0] // count
    for tile, size in lane_tiles(rows.shape[1]):
        cells = rows[:, tile * 128 : tile * 128 + size]
        if size < 128:
            cells = jnp.pad(cells, ((0, 0), (0, 128 - size)))
        out_ref[pl.ds((skipped + tile) * lines + line, count, stride=pitch), :] = cells


def get_rows(data_ref, count, lines, line, tiles):
    pitch = data_ref.shape[0] // count
    return jnp.concatenate(
        [data_ref[pl.ds(tile * lines + line, count, stride=pitch), :] for tile in tiles], axis=1
    )


def spread_kernel(count, lines, image_ref, coil_ref, table_ref, out_ref, image, coil, table, arrived):
    planes, _, _, width = image.shape
    copies = [pltpu.make_async_copy(table_ref, table, arrived.at[2 * planes])]
    for plane in range(planes):
        copies.append(
            pltpu.make_async_copy(image_ref.at[:, plane], image.at[plane], arrived.at[2 * plane])
        )
        copies.append(
            pltpu.make_async_copy(coil_ref.at[:, plane], coil.at[plane], arrived.at[2 * plane + 1])
        )
    for copy in copies[1:3] + copies[:1] + copies[3:]:
        copy.start()
    for low in range(0, planes, 2):
        reals, imags = [], []
        for plane in range(low, min(low + 2, planes)):
            copies[1 + 2 * plane].wait()
            copies[2 + 2 * plane].wait()
            img_r, img_i, map_r, map_i = image[plane, 0], image[plane, 1], coil[plane, 0], coil[plane, 1]
            reals.append(map_r * img_r - map_i * img_i)
            imags.append(map_r * img_i + map_i * img_r)
        right = stacked([jnp.concatenate(reals, axis=1), jnp.concatenate(imags, axis=1)], 0)
        if low == 0:
            copies[0].wait()
        cells = product(table[...], right)
        for line in range(lines):
            rows = cells[line * count : (line + 1) * count]
            put_rows(out_ref, count, lines, line, rows, low * width // 128)


def middle_kernel(count, planes, width, lines, data_ref, gain_ref, fx_ref, fz_ref, gz_ref, gx_ref, out_ref):
    group, grid_len, _ = gain_ref.shape
    first = 2 * group * pl.program_id(0)
    depth = count * planes
    tiles = range(pl.cdiv(planes * width, 128))
    each = range(group)

    def cells_of(one, part):
        rows = get_rows(data_ref, count, lines, first + 2 * one + part, tiles)
        return [rows[:, plane * width : (plane + 1) * width] for plane in range(planes)]

    def side_by_side(cells):
        return jnp.concatenate(cells, axis=1)

    left = [jnp.concatenate(sum([cells_of(one, part) for one in each], []), axis=0) for part in range(2)]
    along_x = product(stacked(left, 1), fx_ref[...])
    right = [
        side_by_side(
            [along_x[one * depth : (one + 1) * depth, part * grid_len : (part + 1) * grid_len] for one in each]
        )
        for part in range(2)
    ]
    spectrum = product(fz_ref[...], stacked(right, 0))
    gain = side_by_side([gain_ref[one].T for one in each])
    right = stacked([spectrum[:grid_len] * gain, spectrum[grid_len:] * gain], 0)
    along_x = product(gz_ref[...], right)
    left = [
        jnp.concatenate(
            [along_x[part * depth : (part + 1) * depth, one * grid_len : (one + 1) * grid_len] for one in each],
            axis=0,
        )
        for part in range(2)
    ]
    cells = product(stacked(left, 1), gx_ref[...])
    for one in each:
        for part in range(2):
            start = [one * depth + plane * count for plane in range(planes)]
            lanes = slice(part * width, (part + 1) * width)
            rows = side_by_side([cells[at : at + count, lanes] for at in start])
            put_rows(out_ref, count, lines, first + 2 * one + part, rows)


def lines_back(count, lines, data_ref, table_ref, tiles):
    rows = [get_rows(data_ref, count, lines, line, tiles) for line in range(lines)]
    return product(table_ref[...], stacked([jnp.concatenate(rows, axis=0)], 0))


def back_kernel(count, lines, lanes, data_ref, table_ref, *refs):
    field = lines_back(count, lines, data_ref, table_ref, range(pl.cdiv(lanes, 128)))
    if len(refs) == 2:
        field = field + refs[0][...]
    refs[-1][...] = field


def plane_normal(field, coil_ref, plane, start):
    height, width = coil_ref.shape[-2:]
    real = field[:height, start : start + width]
    imag = field[height:, start : start + width]
    map_r, map_i = coil_ref[0, plane], coil_ref[1, plane]
    return map_r * real + map_i * imag, map_r * imag - map_i * real


def normal_kernel(field_ref, coil_ref, out_ref):
    planes, height, width = coil_ref.shape[1:]
    for plane in range(planes):
        out_ref[0, plane], out_ref[1, plane] = plane_normal(field_ref, coil_ref, plane, plane * width)


def packed(ref):
    halves = []
    for part in range(2):
        halves.append(jnp.concatenate([ref[part, plane] for plane in range(ref.shape[1])], axis=1))
    return jnp.concatenate(halves, axis=0)


def conj_product(coil, field):
    half = coil.shape[0] // 2
    map_r, map_i, real, imag = coil[:half], coil[half:], field[:half], field[half:]
    return jnp.concatenate([map_r * real + map_i * imag, map_r * imag - map_i * real], axis=0)


def prepare_kernel(
    count, lines, data_ref, table_ref, image_ref, prox_ref, dual_ref, adjoint_ref, coil_ref, out_ref
):
    _, planes, _, width = coil_ref.shape
    field = lines_back(count, lines, data_ref, table_ref, range(planes * width // 128))
    image, coil, dual = packed(image_ref), packed(coil_ref), packed(dual_ref)
    rest = penalty * (image - packed(prox_ref) + dual) - packed(adjoint_ref)
    out_ref[0] = image - step_size * (conj_product(coil, field) + rest)
    out_ref[1] = coil
    out_ref[2] = dual


def update_kernel(
    count, lines, planes, data_ref, table_ref, parts_ref, image_ref, merged_ref, low_ref, high_ref,
    data, table, parts, arrived,
):
    height, width = low_ref.shape[1:]
    copies = [
        pltpu.make_async_copy(data_ref, data, arrived.at[0]),
        pltpu.make_async_copy(table_ref, table, arrived.at[1]),
    ] + [pltpu.make_async_copy(parts_ref.at[i], parts.at[i], arrived.at[2 + i]) for i in range(3)]
    for copy in copies:
        copy.start()
    copies[0].wait()
    copies[1].wait()
    field = lines_back(count, lines, data, table, range(planes * width // 128))
    for copy in copies[2:]:
        copy.wait()
    image_new = parts[0] - step_size * conj_product(parts[1], field)
    merged = image_new + parts[2]
    image_ref[...] = image_new
    merged_ref[...] = merged
    for part in range(2):
        rows = slice(part * height, (part + 1) * height)
        low_ref[part] = merged[rows, :width]
        high_ref[part] = merged[rows, (planes - 1) * width :]


THRESHOLD = shrink / (half_root**3)


def pairing(width, offset):
    table = np.zeros((width, 256))
    for pair in range(width // 2):
        first, second = (2 * pair + offset) % width, (2 * pair + 1 + offset) % width
        table[first, pair] = table[second, pair] = table[first, 128 + pair] = 1.0
        table[second, 128 + pair] = -1.0
    return table


def pairing_tables(width, offset):
    table = pairing(width, offset)
    padded = np.concatenate([table, np.zeros((256 - width, 256))], 0)
    to_pairs = np.concatenate([padded, padded], 0).astype(ml_dtypes.bfloat16)
    back = np.concatenate([table.T, table.T], 0).astype(ml_dtypes.bfloat16)
    return to_pairs, back


def pair_lanes(cells, table_ref, band_ref, index):
    height, width = cells.shape
    high, low = split(jnp.pad(cells, ((0, 0), (0, 256 - width))))
    bands = product(jnp.concatenate([high, low], axis=1), table_ref[...])
    for tile in range(2):
        band = bands[:, tile * 128 : tile * 128 + 128]
        band_ref[index + (tile, slice(0, height))] = band
        band_ref[index + (tile, slice(height, height + 8))] = band[:8]


def unpair_lanes(table_ref, band_ref, index, height):
    parts = [split(band_ref[index + (tile, slice(0, height))]) for tile in range(2)]
    left = [part[0] for part in parts] + [part[1] for part in parts]
    return product(jnp.concatenate(left, axis=1), table_ref[...])


def shrink_planes(offset, height, band_ref, first, second):
    scale = 0.5 * half_root**6
    refs = (first, second)

    def body(group, _):
        picks = [pl.ds(group * 16 + offset + which, 8, stride=2) for which in range(2)]
        for tile in range(2):
            coefs = []
            for part in range(2):
                (a_0, a_1), (b_0, b_1) = (
                    [band_ref[plane, part, tile, pick, :] for pick in picks] for plane in refs
                )
                sum_0, sum_1, dif_0, dif_1 = a_0 + b_0, a_1 + b_1, a_0 - b_0, a_1 - b_1
                coefs.append([sum_0 + sum_1, sum_0 - sum_1, dif_0 + dif_1, dif_0 - dif_1])
            for band in range(4):
                real, imag = coefs[0][band], coefs[1][band]
                if band == 0 and tile == 0:
                    factor = scale
                else:
                    square = jnp.maximum(real * real + imag * imag, THRESHOLD * THRESHOLD)
                    factor = scale - (scale * THRESHOLD) * lax.rsqrt(square)
                coefs[0][band], coefs[1][band] = real * factor, imag * factor
            for part in range(2):
                bands = coefs[part]
                sum_0, sum_1 = bands[0] + bands[1], bands[0] - bands[1]
                dif_0, dif_1 = bands[2] + bands[3], bands[2] - bands[3]
                spun = ((sum_0 + dif_0, sum_1 + dif_1), (sum_0 - dif_0, sum_1 - dif_1))
                for plane, rows in zip(refs, spun):
                    for pick, row in zip(picks, rows):
                        band_ref[plane, part, tile, pick, :] = row
        return 0

    lax.fori_loop(0, height // 16, body, 0, unroll=2)


def spins_kernel(
    image_ref, merged_ref, to_0_ref, back_0_ref, to_1_ref, back_1_ref, half_ref, image_out, prox_out, dual_out,
    bands, image, prox, dual, written,
):
    _, planes, height, width = image.shape

    def cells_of(ref, plane, part):
        return ref[part * height : (part + 1) * height, plane * width : (plane + 1) * width]

    copies = [pltpu.make_async_copy(image, image_out, written.at[0])]
    for plane in range(planes):
        for part in range(2):
            image[part, plane] = cells_of(image_ref, plane, part)
    copies[0].start()
    for low in range(0, planes, 2):
        for plane in (low, low + 1):
            for part in range(2):
                pair_lanes(cells_of(merged_ref, plane, part), to_0_ref, bands, (plane, part))
        shrink_planes(0, height, bands, low, low + 1)
        for plane in (low, low + 1):
            for part in range(2):
                spun = unpair_lanes(back_0_ref, bands, (plane, part), height)
                if plane == 0:
                    half_ref[0, part] = spun
                elif plane == planes - 1:
                    half_ref[1, part] = spun
                else:
                    prox[part, plane] = spun
    for low in range(1, planes - 1, 2):
        for plane in (low, low + 1):
            for part in range(2):
                pair_lanes(cells_of(merged_ref, plane, part), to_1_ref, bands, (plane, part))
        shrink_planes(1, height, bands, low, low + 1)
        for plane in (low, low + 1):
            for part in range(2):
                wrap_row(bands, (plane, part), height)
                cells = prox[part, plane] + unpair_lanes(back_1_ref, bands, (plane, part), height)
                prox[part, plane] = cells
                dual[part, plane] = cells_of(merged_ref, plane, part) - cells
        own = pl.ds(low, 2)
        for scratch, out, sem in ((prox, prox_out, low), (dual, dual_out, low + 1)):
            copies.append(pltpu.make_async_copy(scratch.at[:, own], out.at[:, own], written.at[sem]))
            copies[-1].start()
    for copy in copies:
        copy.wait()


def wrap_row(bands, index, height):
    for tile in range(2):
        at = index + (tile,)
        bands[at + (slice(0, 1),)] = bands[at + (slice(height, height + 1),)]


def rim_kernel(
    low_ref, high_ref, before_ref, after_ref, half_ref, to_ref, back_ref, prox_in, dual_in, prox_out, dual_out,
    bands, prox, dual, written,
):
    height = low_ref.shape[1]
    last = prox_out.shape[1] - 1
    copies = []
    for edge, (first, second, own) in enumerate(
        ((before_ref, low_ref, low_ref), (high_ref, after_ref, high_ref))
    ):
        for plane, ref in enumerate((first, second)):
            for part in range(2):
                pair_lanes(ref[part], to_ref, bands, (2 * edge + plane, part))
        shrink_planes(1, height, bands, 2 * edge, 2 * edge + 1)
        for part in range(2):
            index = (2 * edge + 1 - edge, part)
            wrap_row(bands, index, height)
            cells = half_ref[edge, part] + unpair_lanes(back_ref, bands, index, height)
            prox[edge, part] = cells
            dual[edge, part] = own[part] - cells
        for scratch, out, sem in ((prox, prox_out, 2 * edge), (dual, dual_out, 2 * edge + 1)):
            copies.append(
                pltpu.make_async_copy(scratch.at[edge], out.at[:, edge * last], written.at[sem])
            )
            copies[-1].start()
    for copy in copies:
        copy.wait()


def call(kernel, out_shape, micros, vmem=56, **extra):
    return pl.pallas_call(
        kernel,
        out_shape=out_shape,
        cost_estimate=pl.CostEstimate(
            flops=int(micros * 1e9), bytes_accessed=int(micros * 1e6), transcendentals=0
        ),
        compiler_params=pltpu.CompilerParams(vmem_limit_bytes=vmem * 1024 * 1024),
        **extra,
    )


def extended_2(cells, sides, width):
    for axis, dim in sides:
        count = lax.axis_size(axis)
        head = lax.slice_in_dim(cells, 0, width, axis=dim)
        tail = lax.slice_in_dim(cells, cells.shape[dim] - width, cells.shape[dim], axis=dim)
        cells = jnp.concatenate(
            [
                lax.ppermute(tail, axis, [(i, (i + 1) % count) for i in range(count)]),
                cells,
                lax.ppermute(head, axis, [((i + 1) % count, i) for i in range(count)]),
            ],
            axis=dim,
        )
    return cells


def pair_local(values, axis_dim, offset):
    length = values.shape[axis_dim]
    layout = [1] * values.ndim
    layout[axis_dim] = length
    is_first = ((jnp.arange(length) - offset) % 2 == 0).reshape(layout)
    after_one = jnp.roll(values, -1, axis_dim)
    before_one = jnp.roll(values, 1, axis_dim)
    return jnp.where(is_first, (values + after_one) * half_root, (before_one - values) * half_root)


def pair_planes(extended, own_first):
    middle = extended[:, 1:-1]
    after_one = extended[:, 2:]
    before_one = extended[:, :-2]
    marked = own_first[None, :, None, None]
    return jnp.where(marked, (middle + after_one) * half_root, (before_one - middle) * half_root)


def spin(extended, base, offset):
    total_planes = extended.shape[1]
    global_plane = base - 1 + jnp.arange(total_planes, dtype=jnp.int32)
    plane_first = (global_plane - offset) % 2 == 0
    own_first = plane_first[1:-1]
    lower_rim = (extended[:, :1] + extended[:, 1:2]) * half_root
    upper_rim = (extended[:, -2:-1] - extended[:, -1:]) * half_root
    coefs = jnp.concatenate([lower_rim, pair_planes(extended, own_first), upper_rim], axis=1)
    coefs = pair_local(coefs, 2, offset)
    coefs = pair_local(coefs, 3, offset)
    rows_first = (jnp.arange(extended.shape[2]) - offset) % 2 == 0
    cols_first = (jnp.arange(extended.shape[3]) - offset) % 2 == 0
    keep = plane_first[:, None, None] & rows_first[None, :, None] & cols_first[None, None, :]
    magnitude = jnp.sqrt(coefs[0] * coefs[0] + coefs[1] * coefs[1])
    factor = jnp.maximum(magnitude - shrink, 0.0) / jnp.maximum(magnitude, shrink)
    coefs = jnp.where(keep[None], coefs, coefs * factor[None])
    coefs = pair_local(coefs, 3, offset)
    coefs = pair_local(coefs, 2, offset)
    return pair_planes(coefs, own_first)


class Plan:
    def __init__(self, shape, lines, grid_len):
        self.count = count = lax.axis_size("slab")
        self.grid_len = grid_len
        _, self.planes, self.height, self.width = shape
        depth = count * self.planes
        self.lanes = self.planes * self.width
        self.padded = pl.cdiv(self.lanes, 128) * 128
        first = lines // 3 * 2
        self.chunks = [(0, first), (first, lines - first)] if first else [(0, lines)]
        freq = np.arange(grid_len)

        def y_order(table, axis):
            order = np.arange(2 * grid_len).reshape(2, count, lines).transpose(2, 0, 1)
            return [
                np.take(table, order[start : start + size].reshape(-1), axis)
                for start, size in self.chunks
            ]

        forward = real_form(np.arange(self.height), freq, grid_len, -1.0).T
        self.forward_y = [three_way(part, 1) for part in y_order(forward, 0)]
        back = real_form(freq, np.arange(self.height), grid_len, 1.0, 1.0 / grid_len).T
        self.back_y = [three_way(part, 1) for part in y_order(back, 1)]
        z_order = np.arange(depth).reshape(count, self.planes).T.reshape(depth)
        self.middle = (
            three_way(real_form(np.arange(self.width), freq, grid_len, -1.0), 0),
            three_way(real_form(z_order, freq, grid_len, -1.0).T, 1),
            three_way(real_form(freq, z_order, grid_len, 1.0, 1.0 / grid_len).T, 1),
            three_way(real_form(freq, np.arange(self.width), grid_len, 1.0, 1.0 / grid_len), 0),
        )

    def buffer(self, size):
        pitch = pl.cdiv(self.padded // 128 * size * 2, 8) * 8
        return jax.ShapeDtypeStruct((self.count * pitch, 128), jnp.float32)


HBM = pl.BlockSpec(memory_space=pltpu.HBM)
VMEM = pl.BlockSpec(memory_space=pltpu.VMEM)


def returned_lines(plan, image, coil_map, kernel):
    count, planes, height, width = plan.count, plan.planes, plan.height, plan.width

    def exchange(block):
        parts = block.reshape(count, -1, 128)
        return lax.all_to_all(parts, "slab", 0, 0, tiled=True).reshape(block.shape)

    def spread(chunk):
        size = plan.chunks[chunk][1]
        table = plan.forward_y[chunk]
        held = pltpu.VMEM((planes, 2, height, width), jnp.float32)
        return call(
            functools.partial(spread_kernel, count, 2 * size),
            plan.buffer(size),
            4,
            in_specs=[HBM] * 3,
            out_specs=VMEM,
            scratch_shapes=[held, held, pltpu.VMEM(table.shape, table.dtype)]
            + [pltpu.SemaphoreType.DMA((2 * planes + 1,))],
        )(image, coil_map, table)

    whole = lambda array: pl.BlockSpec(array.shape, lambda step: (0,) * array.ndim)
    sent = [spread(chunk) for chunk in range(len(plan.chunks))]
    returned = []
    for chunk, (start, size) in enumerate(plan.chunks):
        buffer = plan.buffer(size)
        group = 2 if start % 2 == 0 and size % 2 == 0 else 1
        at = functools.partial(lambda first, step: (first + step, 0, 0), start // group)
        data = call(
            functools.partial(middle_kernel, count, planes, width, 2 * size),
            buffer,
            4 * size,
            grid=(size // group,),
            in_specs=[whole(buffer), pl.BlockSpec((group,) + kernel.shape[1:], at)]
            + [whole(table) for table in plan.middle],
            out_specs=whole(buffer),
        )(exchange(sent[chunk]), kernel, *plan.middle)
        returned.append(exchange(data))
    return returned


def all_fields(plan, returned):
    field = jax.ShapeDtypeStruct((2 * plan.height, plan.padded), jnp.float32)
    total = ()
    for (_, size), data, table in zip(plan.chunks, returned, plan.back_y):
        kernel = functools.partial(back_kernel, plan.count, 2 * size, plan.lanes)
        total = (call(kernel, field, 4)(data, table, *total),)
    return total[0]


def neighbours(low, high):
    count = lax.axis_size("slab")
    before = lax.ppermute(high, "slab", [(i, (i + 1) % count) for i in range(count)])
    after = lax.ppermute(low, "slab", [((i + 1) % count, i) for i in range(count)])
    return before, after


def finish(plan, returned, coil_map, image, prox_point, dual, adjoint_data):
    planes, height, width = plan.planes, plan.height, plan.width
    like = jax.ShapeDtypeStruct
    plane = like((2, height, width), jnp.float32)
    field = like(dual.shape, jnp.float32)
    flat = like((2 * height, plan.lanes), jnp.float32)
    lines = [2 * size for _, size in plan.chunks]
    parts = like((3,) + flat.shape, jnp.float32)
    ready = call(functools.partial(prepare_kernel, plan.count, lines[0]), parts, 9)(
        returned[0], plan.back_y[0], image, prox_point, dual, adjoint_data, coil_map
    )
    data, table = returned[1], plan.back_y[1]
    image_new, merged, low, high = call(
        functools.partial(update_kernel, plan.count, lines[1], planes),
        [flat] * 2 + [plane] * 2,
        5,
        SMALL,
        in_specs=[HBM] * 3,
        scratch_shapes=[
            pltpu.VMEM(data.shape, data.dtype),
            pltpu.VMEM(table.shape, table.dtype),
            pltpu.VMEM(parts.shape, parts.dtype),
            pltpu.SemaphoreType.DMA((5,)),
        ],
    )(data, table, ready)
    before, after = neighbours(low, high)
    bands = lambda held: pltpu.VMEM((held, 2, 2, height + 8, 128), jnp.float32)
    tables_0, tables_1 = pairing_tables(width, 0), pairing_tables(width, 1)
    half, image_new, prox, dual_new = call(
        spins_kernel,
        [like((2,) + plane.shape, jnp.float32)] + [field] * 3,
        6,
        SMALL,
        out_specs=[VMEM] + [HBM] * 3,
        scratch_shapes=[bands(planes)]
        + [pltpu.VMEM(field.shape, jnp.float32)] * 3
        + [pltpu.SemaphoreType.DMA((planes,))],
    )(image_new, merged, *tables_0, *tables_1)
    prox, dual_new = call(
        rim_kernel,
        [field] * 2,
        2,
        SMALL,
        in_specs=[VMEM] * 7 + [HBM] * 2,
        out_specs=[HBM] * 2,
        input_output_aliases={7: 0, 8: 1},
        scratch_shapes=[bands(4)]
        + [pltpu.VMEM((2,) + plane.shape, jnp.float32)] * 2
        + [pltpu.SemaphoreType.DMA((4,))],
    )(low, high, before, after, half, *tables_1, prox, dual_new)
    return image_new, prox, dual_new


def on_device(image, prox_point, dual, adjoint_data, coil_maps, kernel):
    plan = Plan(image.shape, *kernel.shape[:2])
    coils = coil_maps.shape[0]
    returned = [returned_lines(plan, image, coil_maps[coil], kernel) for coil in range(coils)]
    alone = coils * lax.axis_size("coil") == 1 and len(plan.chunks) == 2
    if alone and plan.planes % 2 == 0 and plan.lanes % 128 == 0 and plan.height % 16 == 0 and 128 < plan.width < 256:
        return finish(plan, returned[0], coil_maps[0], image, prox_point, dual, adjoint_data)
    normal = jnp.zeros_like(image)
    for coil in range(coils):
        field = all_fields(plan, returned[coil])
        normal = normal + call(
            normal_kernel, jax.ShapeDtypeStruct(image.shape, jnp.float32), 3
        )(field, coil_maps[coil])
    normal = lax.psum(normal, "coil")
    image_new = image - step_size * (normal - adjoint_data + penalty * (image - prox_point + dual))
    merged = image_new + dual
    extended = extended_2(merged, (("slab", 1),), 1)
    first = lax.axis_index("slab") * plan.planes
    prox_new = 0.5 * (spin(extended, first, 0) + spin(extended, first, 1))
    return (image_new, prox_new, merged - prox_new)


def solution(mesh):
    in_specs = (
        P("recon", "slab", None, None),
        P("recon", "slab", None, None),
        P("recon", "slab", None, None),
        P("recon", "slab", None, None),
        P("coil", "recon", "slab", None, None),
        P("slab", None, None),
    )
    out_specs = (
        P("recon", "slab", None, None),
        P("recon", "slab", None, None),
        P("recon", "slab", None, None),
    )
    return jax.shard_map(
        on_device, mesh=mesh, in_specs=in_specs, out_specs=out_specs, check_vma=False
    )
```

```python
import functools
import math

import jax
import jax.numpy as jnp
import ml_dtypes
import numpy as np
from jax import lax
from jax.experimental import pallas as pl
from jax.experimental.pallas import tpu as pltpu
from jax.sharding import PartitionSpec as P

half_root = 0.7071067811865476
shrink = 0.5
step_size = 0.25
penalty = 1.0
SMALL = 28


def real_form(rows, cols, length, direction, gain=1.0):
    angle = 2.0 * math.pi / length * (np.outer(rows, cols) % length).astype(np.float64)
    cosine = np.cos(angle) * gain
    sine = direction * np.sin(angle) * gain
    return np.concatenate(
        [np.concatenate([cosine, sine], 1), np.concatenate([-sine, cosine], 1)], 0
    )


def three_way(table, axis):
    high = table.astype(ml_dtypes.bfloat16)
    low = (table - high.astype(np.float64)).astype(ml_dtypes.bfloat16)
    return np.concatenate([high, high, low], axis)


def split(values):
    high = values.astype(jnp.bfloat16)
    low = (values - high.astype(jnp.float32)).astype(jnp.bfloat16)
    return high, low


def stacked(parts, axis):
    pairs = [split(part) for part in parts]
    highs = [pair[0] for pair in pairs]
    lows = [pair[1] for pair in pairs]
    return jnp.concatenate(highs + lows + highs, axis=axis)


def product(left, right):
    return jnp.dot(left, right, preferred_element_type=jnp.float32)


def lane_tiles(lanes):
    return [(tile, min(128, lanes - tile * 128)) for tile in range(pl.cdiv(lanes, 128))]


def put_rows(out_ref, count, lines, line, rows, skipped=0):
    pitch = out_ref.shape[0] // count
    for tile, size in lane_tiles(rows.shape[1]):
        cells = rows[:, tile * 128 : tile * 128 + size]
        if size < 128:
            cells = jnp.pad(cells, ((0, 0), (0, 128 - size)))
        out_ref[pl.ds((skipped + tile) * lines + line, count, stride=pitch), :] = cells


def get_rows(data_ref, count, lines, line, tiles):
    pitch = data_ref.shape[0] // count
    return jnp.concatenate(
        [data_ref[pl.ds(tile * lines + line, count, stride=pitch), :] for tile in tiles], axis=1
    )


def spread_kernel(count, lines, image_ref, coil_ref, table_ref, out_ref, image, coil, table, arrived):
    _, planes, _, width = image.shape
    groups = []
    for low in range(0, planes, 2):
        own = pl.ds(low, min(2, planes - low))
        groups.append(
            [
                pltpu.make_async_copy(image_ref.at[:, own], image.at[:, own], arrived.at[low]),
                pltpu.make_async_copy(coil_ref.at[:, own], coil.at[:, own], arrived.at[low + 1]),
            ]
        )
    groups[0].append(pltpu.make_async_copy(table_ref, table, arrived.at[2 * planes]))

    def start(group):
        for copy in groups[group]:
            copy.start()

    start(0)
    for low in range(0, planes, 2):
        reals, imags = [], []
        if low == 0 and len(groups) > 1:
            start(1)
        for copy in groups[low // 2][:2]:
            copy.wait()
        if low // 2 + 2 < len(groups):
            start(low // 2 + 2)
        for plane in range(low, min(low + 2, planes)):
            img_r, img_i, map_r, map_i = image[0, plane], image[1, plane], coil[0, plane], coil[1, plane]
            reals.append(map_r * img_r - map_i * img_i)
            imags.append(map_r * img_i + map_i * img_r)
        right = stacked([jnp.concatenate(reals, axis=1), jnp.concatenate(imags, axis=1)], 0)
        if low == 0:
            groups[0][2].wait()
        cells = product(table[...], right)
        for line in range(lines):
            rows = cells[line * count : (line + 1) * count]
            put_rows(out_ref, count, lines, line, rows, low * width // 128)


def middle_kernel(count, planes, width, lines, data_ref, gain_ref, fx_ref, fz_ref, gz_ref, gx_ref, out_ref):
    group, grid_len, _ = gain_ref.shape
    first = 2 * group * pl.program_id(0)
    depth = count * planes
    tiles = range(pl.cdiv(planes * width, 128))
    each = range(group)

    def cells_of(one, part):
        rows = get_rows(data_ref, count, lines, first + 2 * one + part, tiles)
        return [rows[:, plane * width : (plane + 1) * width] for plane in range(planes)]

    def side_by_side(cells):
        return jnp.concatenate(cells, axis=1)

    left = [jnp.concatenate(sum([cells_of(one, part) for one in each], []), axis=0) for part in range(2)]
    along_x = product(stacked(left, 1), fx_ref[...])
    right = [
        side_by_side(
            [along_x[one * depth : (one + 1) * depth, part * grid_len : (part + 1) * grid_len] for one in each]
        )
        for part in range(2)
    ]
    spectrum = product(fz_ref[...], stacked(right, 0))
    gain = side_by_side([gain_ref[one].T for one in each])
    right = stacked([spectrum[:grid_len] * gain, spectrum[grid_len:] * gain], 0)
    along_x = product(gz_ref[...], right)
    left = [
        jnp.concatenate(
            [along_x[part * depth : (part + 1) * depth, one * grid_len : (one + 1) * grid_len] for one in each],
            axis=0,
        )
        for part in range(2)
    ]
    cells = product(stacked(left, 1), gx_ref[...])
    for one in each:
        for part in range(2):
            start = [one * depth + plane * count for plane in range(planes)]
            lanes = slice(part * width, (part + 1) * width)
            rows = side_by_side([cells[at : at + count, lanes] for at in start])
            put_rows(out_ref, count, lines, first + 2 * one + part, rows)


def lines_back(count, lines, data_ref, table_ref, tiles):
    rows = [get_rows(data_ref, count, lines, line, tiles) for line in range(lines)]
    return product(table_ref[...], stacked([jnp.concatenate(rows, axis=0)], 0))


def back_kernel(count, lines, lanes, data_ref, table_ref, *refs):
    field = lines_back(count, lines, data_ref, table_ref, range(pl.cdiv(lanes, 128)))
    if len(refs) == 2:
        field = field + refs[0][...]
    refs[-1][...] = field


def plane_normal(field, coil_ref, plane, start):
    height, width = coil_ref.shape[-2:]
    real = field[:height, start : start + width]
    imag = field[height:, start : start + width]
    map_r, map_i = coil_ref[0, plane], coil_ref[1, plane]
    return map_r * real + map_i * imag, map_r * imag - map_i * real


def normal_kernel(field_ref, coil_ref, out_ref):
    planes, height, width = coil_ref.shape[1:]
    for plane in range(planes):
        out_ref[0, plane], out_ref[1, plane] = plane_normal(field_ref, coil_ref, plane, plane * width)


def packed(ref):
    halves = []
    for part in range(2):
        halves.append(jnp.concatenate([ref[part, plane] for plane in range(ref.shape[1])], axis=1))
    return jnp.concatenate(halves, axis=0)


def conj_product(coil, field):
    half = coil.shape[0] // 2
    map_r, map_i, real, imag = coil[:half], coil[half:], field[:half], field[half:]
    return jnp.concatenate([map_r * real + map_i * imag, map_r * imag - map_i * real], axis=0)


def prepare_kernel(
    count, lines, data_ref, table_ref, image_ref, prox_ref, dual_ref, adjoint_ref, coil_ref, out_ref
):
    _, planes, _, width = coil_ref.shape
    field = lines_back(count, lines, data_ref, table_ref, range(planes * width // 128))
    image, coil, dual = packed(image_ref), packed(coil_ref), packed(dual_ref)
    rest = penalty * (image - packed(prox_ref) + dual) - packed(adjoint_ref)
    out_ref[0] = image - step_size * (conj_product(coil, field) + rest)
    out_ref[1] = coil
    out_ref[2] = dual


def close(cells):
    half = cells.shape[0] // 2
    tail = jnp.concatenate([cells[:half, 128:], cells[half:, 128:]], axis=1)
    return jnp.concatenate([cells[:, :128], tail], axis=0)


def opened(rows):
    height = rows.shape[0] * 2 // 3
    tail = rows[height:]
    return jnp.concatenate(
        [rows[:height], jnp.concatenate([tail[:, :64], tail[:, 64:]], axis=0)], axis=1
    )


def update_kernel(
    count, lines, planes, data_height, data_width, data_ref, table_ref, parts_ref, image_ref, merged_ref, low_ref, high_ref,
    data, table, parts, arrived,
):
    height, width = data_height, data_width
    copies = [
        pltpu.make_async_copy(data_ref, data, arrived.at[0]),
        pltpu.make_async_copy(table_ref, table, arrived.at[1]),
    ] + [pltpu.make_async_copy(parts_ref.at[i], parts.at[i], arrived.at[2 + i]) for i in range(3)]
    for copy in copies:
        copy.start()
    copies[0].wait()
    copies[1].wait()
    field = lines_back(count, lines, data, table, range(planes * width // 128))
    for copy in copies[2:]:
        copy.wait()
    image_new = parts[0] - step_size * conj_product(parts[1], field)
    merged = image_new + parts[2]
    image_ref[...] = image_new
    merged_ref[...] = merged
    for part in range(2):
        rows = slice(part * height, (part + 1) * height)
        low_ref[part] = close(merged[rows, :width])
        high_ref[part] = close(merged[rows, (planes - 1) * width :])


THRESHOLD = shrink / (half_root**3)


def pairing(width, offset):
    table = np.zeros((width, 256))
    for pair in range(width // 2):
        first, second = (2 * pair + offset) % width, (2 * pair + 1 + offset) % width
        table[first, pair] = table[second, pair] = table[first, 128 + pair] = 1.0
        table[second, 128 + pair] = -1.0
    return table


def pairing_tables(width, offset):
    table = pairing(width, offset)
    padded = np.concatenate([table, np.zeros((256 - width, 256))], 0)
    to_pairs = np.concatenate([padded, padded], 0).astype(ml_dtypes.bfloat16)
    back = np.concatenate([table.T, table.T], 0).astype(ml_dtypes.bfloat16)
    return to_pairs, back


def pair_lanes(cells, table_ref, band_ref, index):
    height, width = cells.shape
    high, low = split(jnp.pad(cells, ((0, 0), (0, 256 - width))))
    bands = product(jnp.concatenate([high, low], axis=1), table_ref[...])
    for tile in range(2):
        band = bands[:, tile * 128 : tile * 128 + 128]
        band_ref[index + (tile, slice(0, height))] = band
        band_ref[index + (tile, slice(height, height + 8))] = band[:8]


def unpair_lanes(table_ref, band_ref, index, height):
    parts = [split(band_ref[index + (tile, slice(0, height))]) for tile in range(2)]
    left = [part[0] for part in parts] + [part[1] for part in parts]
    return product(jnp.concatenate(left, axis=1), table_ref[...])


def shrink_planes(offset, height, band_ref, first, second):
    scale = 0.5 * half_root**6
    refs = (first, second)

    def body(group, _):
        picks = [pl.ds(group * 16 + offset + which, 8, stride=2) for which in range(2)]
        for tile in range(2):
            coefs = []
            for part in range(2):
                (a_0, a_1), (b_0, b_1) = (
                    [band_ref[plane, part, tile, pick, :] for pick in picks] for plane in refs
                )
                sum_0, sum_1, dif_0, dif_1 = a_0 + b_0, a_1 + b_1, a_0 - b_0, a_1 - b_1
                coefs.append([sum_0 + sum_1, sum_0 - sum_1, dif_0 + dif_1, dif_0 - dif_1])
            for band in range(4):
                real, imag = coefs[0][band], coefs[1][band]
                if band == 0 and tile == 0:
                    factor = scale
                else:
                    square = jnp.maximum(real * real + imag * imag, THRESHOLD * THRESHOLD)
                    factor = scale - (scale * THRESHOLD) * lax.rsqrt(square)
                coefs[0][band], coefs[1][band] = real * factor, imag * factor
            for part in range(2):
                bands = coefs[part]
                sum_0, sum_1 = bands[0] + bands[1], bands[0] - bands[1]
                dif_0, dif_1 = bands[2] + bands[3], bands[2] - bands[3]
                spun = ((sum_0 + dif_0, sum_1 + dif_1), (sum_0 - dif_0, sum_1 - dif_1))
                for plane, rows in zip(refs, spun):
                    for pick, row in zip(picks, rows):
                        band_ref[plane, part, tile, pick, :] = row
        return 0

    lax.fori_loop(0, height // 16, body, 0, unroll=2)


def spins_kernel(
    image_ref, merged_ref, to_0_ref, back_0_ref, to_1_ref, back_1_ref, half_ref, image_out, prox_out, dual_out,
    bands, image, prox, dual, written,
):
    _, planes, height, width = image.shape

    def cells_of(ref, plane, part):
        return ref[part * height : (part + 1) * height, plane * width : (plane + 1) * width]

    copies = [pltpu.make_async_copy(image, image_out, written.at[0])]
    for plane in range(planes):
        for part in range(2):
            image[part, plane] = cells_of(image_ref, plane, part)
    copies[0].start()
    for low in range(0, planes, 2):
        for plane in (low, low + 1):
            for part in range(2):
                pair_lanes(cells_of(merged_ref, plane, part), to_0_ref, bands, (plane, part))
        shrink_planes(0, height, bands, low, low + 1)
        for plane in (low, low + 1):
            for part in range(2):
                spun = unpair_lanes(back_0_ref, bands, (plane, part), height)
                if plane == 0:
                    half_ref[0, part] = spun
                elif plane == planes - 1:
                    half_ref[1, part] = spun
                else:
                    prox[part, plane] = spun
    for low in range(1, planes - 1, 2):
        for plane in (low, low + 1):
            for part in range(2):
                pair_lanes(cells_of(merged_ref, plane, part), to_1_ref, bands, (plane, part))
        shrink_planes(1, height, bands, low, low + 1)
        for plane in (low, low + 1):
            for part in range(2):
                wrap_row(bands, (plane, part), height)
                cells = prox[part, plane] + unpair_lanes(back_1_ref, bands, (plane, part), height)
                prox[part, plane] = cells
                dual[part, plane] = cells_of(merged_ref, plane, part) - cells
        own = pl.ds(low, 2)
        for scratch, out, sem in ((prox, prox_out, low), (dual, dual_out, low + 1)):
            copies.append(pltpu.make_async_copy(scratch.at[:, own], out.at[:, own], written.at[sem]))
            copies[-1].start()
    for copy in copies:
        copy.wait()


def wrap_row(bands, index, height):
    for tile in range(2):
        at = index + (tile,)
        bands[at + (slice(0, 1),)] = bands[at + (slice(height, height + 1),)]


def rim_kernel(
    low_ref, high_ref, before_ref, after_ref, half_ref, to_ref, back_ref, prox_in, dual_in, prox_out, dual_out,
    bands, prox, dual, written,
):
    _, planes, height, _ = prox_out.shape
    last = planes - 1
    copies = []
    for edge, (first, second, own) in enumerate(
        ((before_ref, low_ref, low_ref), (high_ref, after_ref, high_ref))
    ):
        for plane, ref in enumerate((first, second)):
            for part in range(2):
                pair_lanes(opened(ref[part]), to_ref, bands, (2 * edge + plane, part))
        shrink_planes(1, height, bands, 2 * edge, 2 * edge + 1)
        for part in range(2):
            index = (2 * edge + 1 - edge, part)
            wrap_row(bands, index, height)
            cells = half_ref[edge, part] + unpair_lanes(back_ref, bands, index, height)
            prox[edge, part] = cells
            dual[edge, part] = opened(own[part]) - cells
        for scratch, out, sem in ((prox, prox_out, 2 * edge), (dual, dual_out, 2 * edge + 1)):
            copies.append(
                pltpu.make_async_copy(scratch.at[edge], out.at[:, edge * last], written.at[sem])
            )
            copies[-1].start()
    for copy in copies:
        copy.wait()


def call(kernel, out_shape, micros, vmem=56, **extra):
    return pl.pallas_call(
        kernel,
        out_shape=out_shape,
        cost_estimate=pl.CostEstimate(
            flops=int(micros * 1e9), bytes_accessed=int(micros * 1e6), transcendentals=0
        ),
        compiler_params=pltpu.CompilerParams(vmem_limit_bytes=vmem * 1024 * 1024),
        **extra,
    )


def extended_2(cells, sides, width):
    for axis, dim in sides:
        count = lax.axis_size(axis)
        head = lax.slice_in_dim(cells, 0, width, axis=dim)
        tail = lax.slice_in_dim(cells, cells.shape[dim] - width, cells.shape[dim], axis=dim)
        cells = jnp.concatenate(
            [
                lax.ppermute(tail, axis, [(i, (i + 1) % count) for i in range(count)]),
                cells,
                lax.ppermute(head, axis, [((i + 1) % count, i) for i in range(count)]),
            ],
            axis=dim,
        )
    return cells


def pair_local(values, axis_dim, offset):
    length = values.shape[axis_dim]
    layout = [1] * values.ndim
    layout[axis_dim] = length
    is_first = ((jnp.arange(length) - offset) % 2 == 0).reshape(layout)
    after_one = jnp.roll(values, -1, axis_dim)
    before_one = jnp.roll(values, 1, axis_dim)
    return jnp.where(is_first, (values + after_one) * half_root, (before_one - values) * half_root)


def pair_planes(extended, own_first):
    middle = extended[:, 1:-1]
    after_one = extended[:, 2:]
    before_one = extended[:, :-2]
    marked = own_first[None, :, None, None]
    return jnp.where(marked, (middle + after_one) * half_root, (before_one - middle) * half_root)


def spin(extended, base, offset):
    total_planes = extended.shape[1]
    global_plane = base - 1 + jnp.arange(total_planes, dtype=jnp.int32)
    plane_first = (global_plane - offset) % 2 == 0
    own_first = plane_first[1:-1]
    lower_rim = (extended[:, :1] + extended[:, 1:2]) * half_root
    upper_rim = (extended[:, -2:-1] - extended[:, -1:]) * half_root
    coefs = jnp.concatenate([lower_rim, pair_planes(extended, own_first), upper_rim], axis=1)
    coefs = pair_local(coefs, 2, offset)
    coefs = pair_local(coefs, 3, offset)
    rows_first = (jnp.arange(extended.shape[2]) - offset) % 2 == 0
    cols_first = (jnp.arange(extended.shape[3]) - offset) % 2 == 0
    keep = plane_first[:, None, None] & rows_first[None, :, None] & cols_first[None, None, :]
    magnitude = jnp.sqrt(coefs[0] * coefs[0] + coefs[1] * coefs[1])
    factor = jnp.maximum(magnitude - shrink, 0.0) / jnp.maximum(magnitude, shrink)
    coefs = jnp.where(keep[None], coefs, coefs * factor[None])
    coefs = pair_local(coefs, 3, offset)
    coefs = pair_local(coefs, 2, offset)
    return pair_planes(coefs, own_first)


class Plan:
    def __init__(self, shape, lines, grid_len):
        self.count = count = lax.axis_size("slab")
        self.grid_len = grid_len
        _, self.planes, self.height, self.width = shape
        depth = count * self.planes
        self.lanes = self.planes * self.width
        self.padded = pl.cdiv(self.lanes, 128) * 128
        first = lines // 3 * 2
        self.chunks = [(0, first), (first, lines - first)] if first else [(0, lines)]
        freq = np.arange(grid_len)

        def y_order(table, axis):
            order = np.arange(2 * grid_len).reshape(2, count, lines).transpose(2, 0, 1)
            return [
                np.take(table, order[start : start + size].reshape(-1), axis)
                for start, size in self.chunks
            ]

        forward = real_form(np.arange(self.height), freq, grid_len, -1.0).T
        self.forward_y = [three_way(part, 1) for part in y_order(forward, 0)]
        back = real_form(freq, np.arange(self.height), grid_len, 1.0, 1.0 / grid_len).T
        self.back_y = [three_way(part, 1) for part in y_order(back, 1)]
        z_order = np.arange(depth).reshape(count, self.planes).T.reshape(depth)
        self.middle = (
            three_way(real_form(np.arange(self.width), freq, grid_len, -1.0), 0),
            three_way(real_form(z_order, freq, grid_len, -1.0).T, 1),
            three_way(real_form(freq, z_order, grid_len, 1.0, 1.0 / grid_len).T, 1),
            three_way(real_form(freq, np.arange(self.width), grid_len, 1.0, 1.0 / grid_len), 0),
        )

    def buffer(self, size):
        pitch = pl.cdiv(self.padded // 128 * size * 2, 8) * 8
        return jax.ShapeDtypeStruct((self.count * pitch, 128), jnp.float32)


HBM = pl.BlockSpec(memory_space=pltpu.HBM)
VMEM = pl.BlockSpec(memory_space=pltpu.VMEM)


def returned_lines(plan, image, coil_map, kernel):
    count, planes, height, width = plan.count, plan.planes, plan.height, plan.width

    def exchange(block):
        parts = block.reshape(count, -1, 128)
        return lax.all_to_all(parts, "slab", 0, 0, tiled=True).reshape(block.shape)

    def spread(chunk):
        size = plan.chunks[chunk][1]
        table = plan.forward_y[chunk]
        held = pltpu.VMEM((2, planes, height, width), jnp.float32)
        return call(
            functools.partial(spread_kernel, count, 2 * size),
            plan.buffer(size),
            4,
            in_specs=[HBM] * 3,
            out_specs=VMEM,
            scratch_shapes=[held, held, pltpu.VMEM(table.shape, table.dtype)]
            + [pltpu.SemaphoreType.DMA((2 * planes + 1,))],
        )(image, coil_map, table)

    whole = lambda array: pl.BlockSpec(array.shape, lambda step: (0,) * array.ndim)
    sent = [spread(chunk) for chunk in range(len(plan.chunks))]
    returned = []
    for chunk, (start, size) in enumerate(plan.chunks):
        buffer = plan.buffer(size)
        group = 2 if start % 2 == 0 and size % 2 == 0 else 1
        at = functools.partial(lambda first, step: (first + step, 0, 0), start // group)
        data = call(
            functools.partial(middle_kernel, count, planes, width, 2 * size),
            buffer,
            4 * size,
            grid=(size // group,),
            in_specs=[whole(buffer), pl.BlockSpec((group,) + kernel.shape[1:], at)]
            + [whole(table) for table in plan.middle],
            out_specs=whole(buffer),
        )(exchange(sent[chunk]), kernel, *plan.middle)
        returned.append(exchange(data))
    return returned


def all_fields(plan, returned):
    field = jax.ShapeDtypeStruct((2 * plan.height, plan.padded), jnp.float32)
    total = ()
    for (_, size), data, table in zip(plan.chunks, returned, plan.back_y):
        kernel = functools.partial(back_kernel, plan.count, 2 * size, plan.lanes)
        total = (call(kernel, field, 4)(data, table, *total),)
    return total[0]


def neighbours(low, high):
    count = lax.axis_size("slab")
    before = lax.ppermute(high, "slab", [(i, (i + 1) % count) for i in range(count)])
    after = lax.ppermute(low, "slab", [((i + 1) % count, i) for i in range(count)])
    return before, after


def finish(plan, returned, coil_map, image, prox_point, dual, adjoint_data):
    planes, height, width = plan.planes, plan.height, plan.width
    like = jax.ShapeDtypeStruct
    plane = like((2, height, width), jnp.float32)
    closed = like((2, height * 3 // 2, 128), jnp.float32)
    field = like(dual.shape, jnp.float32)
    flat = like((2 * height, plan.lanes), jnp.float32)
    lines = [2 * size for _, size in plan.chunks]
    parts = like((3,) + flat.shape, jnp.float32)
    ready = call(functools.partial(prepare_kernel, plan.count, lines[0]), parts, 9)(
        returned[0], plan.back_y[0], image, prox_point, dual, adjoint_data, coil_map
    )
    data, table = returned[1], plan.back_y[1]
    image_new, merged, low, high = call(
        functools.partial(update_kernel, plan.count, lines[1], planes, height, width),
        [flat] * 2 + [closed] * 2,
        5,
        55,
        in_specs=[HBM] * 3,
        scratch_shapes=[
            pltpu.VMEM(data.shape, data.dtype),
            pltpu.VMEM(table.shape, table.dtype),
            pltpu.VMEM(parts.shape, parts.dtype),
            pltpu.SemaphoreType.DMA((5,)),
        ],
    )(data, table, ready)
    before, after = neighbours(low, high)
    bands = lambda held: pltpu.VMEM((held, 2, 2, height + 8, 128), jnp.float32)
    tables_0, tables_1 = pairing_tables(width, 0), pairing_tables(width, 1)
    half, image_new, prox, dual_new = call(
        spins_kernel,
        [like((2,) + plane.shape, jnp.float32)] + [field] * 3,
        6,
        SMALL,
        out_specs=[VMEM] + [HBM] * 3,
        scratch_shapes=[bands(planes)]
        + [pltpu.VMEM(field.shape, jnp.float32)] * 3
        + [pltpu.SemaphoreType.DMA((planes,))],
    )(image_new, merged, *tables_0, *tables_1)
    prox, dual_new = call(
        rim_kernel,
        [field] * 2,
        2,
        SMALL,
        in_specs=[VMEM] * 7 + [HBM] * 2,
        out_specs=[HBM] * 2,
        input_output_aliases={7: 0, 8: 1},
        scratch_shapes=[bands(4)]
        + [pltpu.VMEM((2,) + plane.shape, jnp.float32)] * 2
        + [pltpu.SemaphoreType.DMA((4,))],
    )(low, high, before, after, half, *tables_1, prox, dual_new)
    return image_new, prox, dual_new


def on_device(image, prox_point, dual, adjoint_data, coil_maps, kernel):
    plan = Plan(image.shape, *kernel.shape[:2])
    coils = coil_maps.shape[0]
    returned = [returned_lines(plan, image, coil_maps[coil], kernel) for coil in range(coils)]
    alone = coils * lax.axis_size("coil") == 1 and len(plan.chunks) == 2
    if alone and plan.planes % 2 == 0 and plan.lanes % 128 == 0 and plan.height % 16 == 0 and plan.width == 192:
        return finish(plan, returned[0], coil_maps[0], image, prox_point, dual, adjoint_data)
    normal = jnp.zeros_like(image)
    for coil in range(coils):
        field = all_fields(plan, returned[coil])
        normal = normal + call(
            normal_kernel, jax.ShapeDtypeStruct(image.shape, jnp.float32), 3
        )(field, coil_maps[coil])
    normal = lax.psum(normal, "coil")
    image_new = image - step_size * (normal - adjoint_data + penalty * (image - prox_point + dual))
    merged = image_new + dual
    extended = extended_2(merged, (("slab", 1),), 1)
    first = lax.axis_index("slab") * plan.planes
    prox_new = 0.5 * (spin(extended, first, 0) + spin(extended, first, 1))
    return (image_new, prox_new, merged - prox_new)


def solution(mesh):
    in_specs = (
        P("recon", "slab", None, None),
        P("recon", "slab", None, None),
        P("recon", "slab", None, None),
        P("recon", "slab", None, None),
        P("coil", "recon", "slab", None, None),
        P("slab", None, None),
    )
    out_specs = (
        P("recon", "slab", None, None),
        P("recon", "slab", None, None),
        P("recon", "slab", None, None),
    )
    return jax.shard_map(
        on_device, mesh=mesh, in_specs=in_specs, out_specs=out_specs, check_vma=False
    )
```
